128 devices in a mesh: dp: 16 (over x_lo, z, core), space: 8 (over x_hi, y).
Axes of the slice: x: 4 (x_hi: 2, x_lo: 2; x = x_hi * 2 + x_lo), y: 4, z: 4, core: 2. Of those that a mesh axis runs over, the one named last changes fastest.
Arguments:
- features: bfloat16 [4096, 6272], P(('dp', 'space')), may hold values from -6 to 6
- grad_out: bfloat16 [4096, 6272], P(('dp', 'space')), may hold values from -6 to 6
- wigner: bfloat16 [455, 16384], P(None, ('dp', 'space')), may hold values from -1.5 to 1.5
- sources: int32 [16384], P(('dp', 'space')), may hold values from 0 to 47
- targets: int32 [16384], P(('dp', 'space')), may hold values from 0 to 31
- ghost_index: int32 [128, 2, 8], P(('dp', 'space')), may hold values from 0 to 31
- edge_count: int32 [16, 8], P('dp', 'space'), may hold values from 1 to 128, 768 in all within a row
- mixture: float32 [16, 32], replicated, may hold values from 0.25 to 2
- w_zero: bfloat16 [32, 896, 896], P('dp', 'space'), may hold values from -0.03125 to 0.03125
- w_one: bfloat16 [32, 2, 768, 768], P('dp', None, 'space'), may hold values from -0.02734375 to 0.02734375
- w_two: bfloat16 [32, 2, 640, 640], P('dp', None, 'space'), may hold values from -0.03125 to 0.03125
Outputs:
- updated: bfloat16 [4096, 6272], P(('dp', 'space'))
- grad_features: bfloat16 [4096, 6272], P(('dp', 'space'))
- grad_mix0: bfloat16 [16, 896, 896], P('dp', 'space')
- grad_mix1: bfloat16 [16, 2, 768, 768], P('dp', None, 'space')
- grad_mix2: bfloat16 [16, 2, 640, 640], P('dp', None, 'space')
The draws below stay inside these ranges and needn't reach their ends.
Inputs may be any that keep to these rules, and one draw needn't show every extreme that they name: `edge_count`: the counts of one system sum to 768, and some device of every system has all 128 slots live.
All inputs are finite; a program needn't handle non-finite values.
Results may differ from the reference program's by a relative error of at most 0.015.
Values may be sent and summed in bfloat16 or wider, within the bound.
A program may use at most 128 MiB of HBM per device.

```python
import math
from functools import partial
import jax
import jax.numpy as jnp
import numpy as np
from jax import lax

CHANNELS = 128
LMAX = 6
MMAX = 2
EXPERTS = 32
ATOM_DEV = 32
EDGE_DEV = 128
GHOSTS = 8
NODE_W = 6272
WIG = 455
K0 = 896
K1 = 768
K2 = 640
PARAMS = 2801664
SYSTEMS = 16
ATOMS = 4096
EDGES = 16384
N_DP = 16
N_SPACE = 8
DEVICES = 128


def degree_tables():
    eyes = []
    spreads = []
    for degree in range(LMAX + 1):
        extent = 2 * degree + 1
        eyes.append(np.eye(extent, dtype=np.float32).reshape(-1))
        spreads.append(np.full(extent * extent, 0.6 / np.sqrt(extent), np.float32))
    return (np.concatenate(eyes)[:, None], np.concatenate(spreads)[:, None])


def draw_wigner(key, part):
    key = jax.random.fold_in(key, 11)
    diagonal, spread = degree_tables()
    first_key, second_key = jax.random.split(key)
    noise = jnp.clip(jax.random.normal(first_key, (WIG, EDGES), jnp.float32), -4.0, 4.0)
    center = jax.random.uniform(second_key, (WIG, EDGES), jnp.float32, 0.7, 1.3)
    value = jnp.asarray(diagonal) * center + (1.0 - jnp.asarray(diagonal)) * jnp.asarray(spread) * noise
    return value.astype(jnp.bfloat16)


def place_ends(array, own_key, low, largest):
    longest = array.shape.index(max(array.shape))
    spots = []
    for shift in (0, 1):
        where = [jax.random.randint(jax.random.fold_in(own_key, axis), (), 0, length) for axis, length in enumerate(array.shape)]
        where[longest] = (where[longest] + shift) % array.shape[longest]
        spots.append(tuple(where))
    return array.at[spots[0]].set(low).at[spots[1]].set(largest)


def steps_of(stream_key, shape, cuts, smallest, high):
    factor_of, own = 1.0, jax.random.fold_in(stream_key, 6)
    for axis_at, parts in cuts:
        draws = jnp.exp(jax.random.uniform(jax.random.fold_in(own, axis_at), (parts,), jnp.float32, smallest / len(cuts), high / len(cuts)))
        factor_of = factor_of * jnp.repeat(draws, shape[axis_at] // parts).reshape([-1 if axis == axis_at else 1 for axis in range(len(shape))])
    return factor_of


def length_profile(count, total, limit, lean):
    portions = [(1 << 20) // math.isqrt(rank ** lean) + 1 for rank in range(2, count + 1)]
    rest, given = total - limit - (count - 1), [1] * (count - 1)
    while rest > 0:
        candidates = [i for i in range(count - 1) if given[i] < limit]
        mass, remaining = sum([portions[i] for i in candidates]), rest
        for i in candidates:
            addition = min(limit - given[i], max(1, remaining * portions[i] // mass), rest)
            given[i] = given[i] + addition
            rest = rest - addition
    return np.array([limit] + given)


def uneven_parts(stream_key, count, total, limit, lean):
    if count == 2:
        one = jax.random.randint(stream_key, (), max(1, total - limit), min(limit, total - 1) + 1)
        return jnp.stack([one, total - one])
    lengths = jnp.asarray(length_profile(count, total, limit, lean), jnp.int32)
    pairs = (count - 1) // 2
    source_of, sink = lengths[1:1 + 2 * pairs:2], lengths[2:2 + 2 * pairs:2]
    slack = jnp.minimum(source_of - 1, limit - sink)
    moved = jax.random.randint(jax.random.fold_in(stream_key, 1), (pairs,), 0, 1 << 20) % (slack + 1)
    lengths = lengths.at[1:1 + 2 * pairs:2].set(source_of - moved).at[2:2 + 2 * pairs:2].set(sink + moved)
    return lengths[jax.random.permutation(jax.random.fold_in(stream_key, 2), count)]


def bell_draw(own_key, shape, scale, limit, cuts=(), kind=jnp.bfloat16):
    array = scale * jax.random.normal(own_key, shape, jnp.float32)
    if cuts:
        array = array * steps_of(own_key, shape, cuts, -0.22, 0.18)
    return jnp.clip(array, -limit, limit).astype(kind)


def setup_inputs(seed: int = 0) -> dict:
    key_of = jax.random.split(jax.random.key(seed), 12)
    return {
        "features": bell_draw(key_of[0], (ATOMS, NODE_W), 1.0, 6.0, ((0, 128),)),
        "grad_out": bell_draw(key_of[1], (ATOMS, NODE_W), 1.0, 6.0, ((0, 128),)),
        "wigner": draw_wigner(jax.random.fold_in(key_of[11], 71), 0),
        "sources": place_ends(jax.random.randint(key_of[3], (EDGES,), 0, ATOM_DEV + 2 * GHOSTS), jax.random.fold_in(key_of[3], 1), 0, (ATOM_DEV + 2 * GHOSTS) - 1).astype(jnp.int32),
        "targets": place_ends(jax.random.randint(key_of[4], (EDGES,), 0, ATOM_DEV), jax.random.fold_in(key_of[4], 1), 0, ATOM_DEV - 1).astype(jnp.int32),
        "ghost_index": place_ends(jax.random.randint(key_of[5], (DEVICES, 2, GHOSTS), 0, ATOM_DEV), jax.random.fold_in(key_of[5], 1), 0, ATOM_DEV - 1).astype(jnp.int32),
        "edge_count": jax.vmap(lambda own: uneven_parts(own, N_SPACE, 3 * N_SPACE * EDGE_DEV // 4, EDGE_DEV, 2))(jax.random.split(key_of[6], SYSTEMS)).reshape((SYSTEMS, N_SPACE)).astype(jnp.int32),
        "mixture": jnp.clip(jnp.exp(jax.random.uniform(key_of[7], (SYSTEMS, EXPERTS), jnp.float32, math.log(0.25), math.log(2.0))), 0.25, 2.0),
        "w_zero": bell_draw(key_of[8], (EXPERTS, K0, K0), (K0 * EXPERTS) ** -0.5, 0.03125, ((0, 16), (1, 8))),
        "w_one": bell_draw(key_of[9], (EXPERTS, 2, K1, K1), (2 * K1 * EXPERTS) ** -0.5, 0.02734375, ((0, 16), (2, 8))),
        "w_two": bell_draw(key_of[10], (EXPERTS, 2, K2, K2), (2 * K2 * EXPERTS) ** -0.5, 0.03125, ((0, 16), (2, 8))),
    }


message_scale = 0.25


def degree_start(degree):
    return degree * (2 * degree - 1) * (2 * degree + 1) // 3


def product_of(form, left_side, right_side):
    return jnp.einsum(form, left_side.astype(jnp.float32), right_side.astype(jnp.float32), precision=lax.Precision.HIGHEST)


def rotate_into(wigner, edge_rows):
    row_count = edge_rows.shape[0]
    blocks = []
    for degree in range(LMAX + 1):
        extent = 2 * degree + 1
        kept_order = min(degree, MMAX)
        offset = degree_start(degree)
        matrix = wigner[offset:offset + extent * extent].reshape(extent, extent, row_count)[degree - kept_order:degree + kept_order + 1]
        segment = edge_rows[:, degree * degree * CHANNELS:(degree + 1) * (degree + 1) * CHANNELS].reshape(row_count, extent, CHANNELS)
        blocks.append(product_of('jne,enc->ejc', matrix, segment).astype(jnp.bfloat16))
    return blocks


def rotate_back(wigner, blocks):
    row_count = blocks[0].shape[0]
    pieces = []
    for degree in range(LMAX + 1):
        extent = 2 * degree + 1
        kept_order = min(degree, MMAX)
        offset = degree_start(degree)
        matrix = wigner[offset:offset + extent * extent].reshape(extent, extent, row_count)[degree - kept_order:degree + kept_order + 1]
        pieces.append(product_of('jne,ejc->enc', matrix, blocks[degree]).reshape(row_count, extent * CHANNELS))
    return jnp.concatenate(pieces, 1)


def split_frame(blocks):
    row_count = blocks[0].shape[0]
    frame_zero = jnp.stack([blocks[d][:, min(d, MMAX)] for d in range(LMAX + 1)], 1).reshape(row_count, -1)
    frame_pairs = []
    for order_m in range(1, MMAX + 1):
        plus_part = jnp.stack([blocks[d][:, min(d, MMAX) + order_m] for d in range(order_m, LMAX + 1)], 1).reshape(row_count, -1)
        minus_part = jnp.stack([blocks[d][:, min(d, MMAX) - order_m] for d in range(order_m, LMAX + 1)], 1).reshape(row_count, -1)
        frame_pairs.append((plus_part, minus_part))
    return frame_zero, frame_pairs


def join_frame(frame_zero, frame_pairs):
    row_count = frame_zero.shape[0]
    zero_rows = frame_zero.reshape(row_count, LMAX + 1, CHANNELS)
    reshaped = [(p.reshape(row_count, -1, CHANNELS), q.reshape(row_count, -1, CHANNELS)) for p, q in frame_pairs]
    blocks = []
    for degree in range(LMAX + 1):
        kept_order = min(degree, MMAX)
        row_list = []
        for order_m in range(-kept_order, kept_order + 1):
            if order_m == 0:
                row_list.append(zero_rows[:, degree])
            elif order_m > 0:
                row_list.append(reshaped[order_m - 1][0][:, degree - order_m])
            else:
                row_list.append(reshaped[-order_m - 1][1][:, degree + order_m])
        blocks.append(jnp.stack(row_list, 1))
    return blocks


def convolve(frame_zero, frame_pairs, mix_set):
    out_zero = jnp.dot(frame_zero, mix_set[0], preferred_element_type=jnp.float32).astype(jnp.bfloat16)
    out_pairs = []
    for index_m, (plus_part, minus_part) in enumerate(frame_pairs):
        real_weight = mix_set[index_m + 1][0]
        imag_weight = mix_set[index_m + 1][1]
        out_plus = jnp.dot(plus_part, real_weight, preferred_element_type=jnp.float32) - jnp.dot(minus_part, imag_weight, preferred_element_type=jnp.float32)
        out_minus = jnp.dot(plus_part, imag_weight, preferred_element_type=jnp.float32) + jnp.dot(minus_part, real_weight, preferred_element_type=jnp.float32)
        out_pairs.append((out_plus.astype(jnp.bfloat16), out_minus.astype(jnp.bfloat16)))
    return out_zero, out_pairs


def transposed(left_side, right_side):
    return lax.dot_general(left_side, right_side, (((1,), (1,)), ((), ())), preferred_element_type=jnp.float32)


def outer_product(left_side, right_side):
    return lax.dot_general(left_side, right_side, (((0,), (0,)), ((), ())), preferred_element_type=jnp.float32)


def convolve_back(frame_zero, frame_pairs, mix_set):
    grad_zero = transposed(frame_zero, mix_set[0]).astype(jnp.bfloat16)
    grad_pairs = []
    for index_m, (plus_part, minus_part) in enumerate(frame_pairs):
        real_weight = mix_set[index_m + 1][0]
        imag_weight = mix_set[index_m + 1][1]
        grad_plus = transposed(plus_part, real_weight) + transposed(minus_part, imag_weight)
        grad_minus = transposed(minus_part, real_weight) - transposed(plus_part, imag_weight)
        grad_pairs.append((grad_plus.astype(jnp.bfloat16), grad_minus.astype(jnp.bfloat16)))
    return grad_zero, grad_pairs


def weight_terms(frame_zero, frame_pairs, back_zero, back_pairs, weight_scale):
    result = [(weight_scale * outer_product(frame_zero, back_zero))[None]]
    for (plus_part, minus_part), (back_plus, back_minus) in zip(frame_pairs, back_pairs):
        real_grad = outer_product(plus_part, back_plus) + outer_product(minus_part, back_minus)
        imag_grad = outer_product(plus_part, back_minus) - outer_product(minus_part, back_plus)
        result.append(weight_scale * jnp.stack([real_grad, imag_grad]))
    return tuple(result)


def take_rows(matrix, positions):
    return matrix[positions]


def add_rows(length, values, positions):
    return jnp.zeros((length, values.shape[1]), jnp.float32).at[positions].add(values)


def reference(features, grad_out, wigner, sources, targets, ghost_index, edge_count, mixture, w_zero, w_one, w_two):
    per_group = EXPERTS // N_DP
    experts_flat = jnp.concatenate([w_zero.reshape(EXPERTS, -1), w_one.reshape(EXPERTS, -1), w_two.reshape(EXPERTS, -1)], 1)
    grouped = experts_flat.astype(jnp.float32).reshape(N_DP, per_group, PARAMS)
    weight_scale = float(EDGE_DEV * N_SPACE) ** -0.5
    cut_one = K0 * K0
    cut_two = cut_one + 2 * K1 * K1
    table_rows = ATOM_DEV + 2 * GHOSTS
    slot_count = N_SPACE * EDGE_DEV

    def per_device(values):
        return values.reshape(N_SPACE, EDGE_DEV, -1)

    def one_system(inputs):
        feats_sys, gout_sys, wigner_sys, source_sys, target_sys, ghost_sys, count_sys, mix_row = inputs
        partial_mix = jnp.einsum('ge,gep->gp', mix_row.reshape(N_DP, per_group), grouped, precision=lax.Precision.HIGHEST)
        mixed = jnp.sum(lax.optimization_barrier(partial_mix.astype(jnp.bfloat16)).astype(jnp.float32), 0).astype(jnp.bfloat16)
        mix_set = (mixed[:cut_one].reshape(K0, K0), mixed[cut_one:cut_two].reshape(2, K1, K1), mixed[cut_two:].reshape(2, K2, K2))
        to_next = jax.vmap(take_rows)(feats_sys, ghost_sys[:, 0])
        to_prev = jax.vmap(take_rows)(feats_sys, ghost_sys[:, 1])
        node_table = jnp.concatenate([feats_sys, jnp.roll(to_next, 1, 0), jnp.roll(to_prev, -1, 0)], 1)
        edge_rows = jax.vmap(take_rows)(node_table, source_sys).reshape(slot_count, NODE_W)
        is_live = (jnp.arange(EDGE_DEV, dtype=jnp.int32)[None, :] < count_sys[:, None]).astype(jnp.float32)
        frame_zero, frame_pairs = split_frame(rotate_into(wigner_sys, edge_rows))
        out_zero, out_pairs = convolve(frame_zero, frame_pairs, mix_set)
        messages = rotate_back(wigner_sys, join_frame(out_zero, out_pairs)).astype(jnp.bfloat16)
        live_msgs = messages.reshape(N_SPACE, EDGE_DEV, NODE_W).astype(jnp.float32) * is_live[:, :, None]
        gathered = jax.vmap(partial(add_rows, ATOM_DEV))(live_msgs, target_sys)
        updated = (feats_sys.astype(jnp.float32) + message_scale * gathered).astype(jnp.bfloat16)
        picked = jax.vmap(take_rows)(gout_sys, target_sys).astype(jnp.float32)
        back_msg = (message_scale * picked * is_live[:, :, None]).astype(jnp.bfloat16).reshape(slot_count, NODE_W)
        back_zero, back_pairs = split_frame(rotate_into(wigner_sys, back_msg))
        grad_zero, grad_pairs = convolve_back(back_zero, back_pairs, mix_set)
        dev_pairs = [(per_device(p), per_device(q)) for p, q in frame_pairs]
        dev_back = [(per_device(p), per_device(q)) for p, q in back_pairs]
        dev_terms = jax.vmap(partial(weight_terms, weight_scale=weight_scale))(per_device(frame_zero), dev_pairs, per_device(back_zero), dev_back)
        sums = [jnp.sum(lax.optimization_barrier(term.astype(jnp.bfloat16)).astype(jnp.float32), 0).astype(jnp.bfloat16) for term in dev_terms]
        back_rows = rotate_back(wigner_sys, join_frame(grad_zero, grad_pairs)).astype(jnp.bfloat16)
        table_grad = jax.vmap(partial(add_rows, table_rows))(per_device(back_rows).astype(jnp.float32), source_sys)
        ghost_grad = lax.optimization_barrier(table_grad[:, ATOM_DEV:].astype(jnp.bfloat16)).astype(jnp.float32)
        from_next = jnp.roll(ghost_grad[:, :GHOSTS], -1, 0)
        from_prev = jnp.roll(ghost_grad[:, GHOSTS:], 1, 0)
        combined = gout_sys.astype(jnp.float32) + table_grad[:, :ATOM_DEV]
        combined = combined + jax.vmap(partial(add_rows, ATOM_DEV))(from_next, ghost_sys[:, 0])
        combined = combined + jax.vmap(partial(add_rows, ATOM_DEV))(from_prev, ghost_sys[:, 1])
        return updated, combined.astype(jnp.bfloat16), sums[0][0], sums[1], sums[2]

    inputs = (features.reshape(N_DP, N_SPACE, ATOM_DEV, NODE_W),
              grad_out.reshape(N_DP, N_SPACE, ATOM_DEV, NODE_W),
              jnp.moveaxis(wigner.reshape(WIG, N_DP, N_SPACE * EDGE_DEV), 1, 0),
              sources.reshape(N_DP, N_SPACE, EDGE_DEV),
              targets.reshape(N_DP, N_SPACE, EDGE_DEV),
              ghost_index.reshape(N_DP, N_SPACE, 2, GHOSTS),
              edge_count,
              mixture)
    updated, grad_features, grad_mix0, grad_mix1, grad_mix2 = lax.map(one_system, inputs)
    return (updated.reshape(ATOMS, NODE_W), grad_features.reshape(ATOMS, NODE_W), grad_mix0, grad_mix1, grad_mix2)
```

```python
import functools

import jax
import jax.numpy as jnp
from jax import lax
from jax.experimental import pallas as pl
from jax.experimental.pallas import tpu as pltpu
from jax.sharding import PartitionSpec as P

BF16 = jnp.bfloat16
F32 = jnp.float32
MESH = pl.DeviceIdType.MESH

LMAX = 6
MMAX = 2
EDGES = 128
ATOMS = 32
GHOSTS = 8
WIDTH = 6272
PACK = 3200
WIG = 455
MESSAGE_SCALE = 0.25
WEIGHT_SCALE = 1024.0 ** -0.5

ROWS = (112, 96, 80)
COLS = (896, 768, 640)
MATS = (1, 2, 2)
HALVES = (
    (0, 0, 0, 48, True),
    (0, 0, 48, 64, False),
    (1, 0, 0, 96, True),
    (1, 1, 0, 96, False),
    (2, 0, 0, 80, True),
    (2, 1, 0, 80, False),
)
COPIES = 128


def contract(left, right, left_dim, right_dim):
    return lax.dot_general(
        left, right, (((left_dim,), (right_dim,)), ((), ())), preferred_element_type=F32
    )


def whole(ref, chunk, lead):
    return ref.at[lead] if chunk == 0 else ref.at[(slice(None),) + lead]


def part(ref, half, lead):
    chunk, mat, first, rows, _ = half
    if chunk == 0:
        return ref.at[lead + (pl.ds(first, rows),)]
    return ref.at[(mat,) + lead]


def steps(count, body):
    def step(i, carry):
        body(i)
        return carry

    lax.fori_loop(0, count, step, 0)


def tiles16(i):
    return pl.ds(pl.multiple_of(i * 16, 16), 16)


def kernel(
    mixture, count, features, grad_out, wigner, sources, targets, ghost_col, ghost_row, w0, w1, w2,
    updated, grad_features, out0, out1, out2,
    raw0, raw1, raw2, par0, par1, par2, zf0, zf1, zf2, zl0, zl1, zl2, zr0, zr1, zr2,
    mix0, mix1, mix2, gw0, gw1, gw2, cf0, cf1, cf2, cl0, cl1, cl2, cr0, cr1, cr2,
    cs0, cs1, cs2, cx0, cx1, cx2,
    ghost_send, ghost_recv, back_send, back_recv,
    wig32, blk0, blk1, blk2, blk3, blk4, blk5, blk6,
    table, rows_f, rows_b, v0, v1, v2, d0, d1, d2, s1, s2, t0, t1, t2, u1, u2,
    table_own, table_ghost, send_sem, recv_sem,
):
    w = (w0, w1, w2)
    raw = (raw0, raw1, raw2)
    par = (par0, par1, par2)
    zf, zl, zr = (zf0, zf1, zf2), (zl0, zl1, zl2), (zr0, zr1, zr2)
    mix = (mix0, mix1, mix2)
    gw = (gw0, gw1, gw2)
    cf, cl, cr = (cf0, cf1, cf2), (cl0, cl1, cl2), (cr0, cr1, cr2)
    cs, cx = (cs0, cs1, cs2), (cx0, cx1, cx2)
    out = (out0, out1, out2)
    blocks = (blk0, blk1, blk2, blk3, blk4, blk5, blk6)

    dp, sp = lax.axis_index("dp"), lax.axis_index("space")
    core, z, xl = dp % 2, (dp // 2) % 4, dp // 8
    y, xh = sp % 4, sp // 4
    dp_core = dp + 1 - 2 * core
    dp_x = (1 - xl) * 8 + z * 2 + core
    dp_xc = (1 - xl) * 8 + z * 2 + 1 - core
    sp_x = (1 - xh) * 4 + y

    def at_z(step):
        return xl * 8 + ((z + step) % 4) * 2 + core

    def at_y(step):
        return xh * 4 + (y + step) % 4

    to_core, to_x = (dp_core, sp), (dp_x, sp)
    to_up, to_down = (at_z(1), sp), (at_z(3), sp)
    to_right, to_left = (dp, at_y(1)), (dp, at_y(3))
    to_far = (dp, sp_x)
    to_next, to_prev = (dp, (sp + 1) % 8), (dp, (sp + 7) % 8)
    partners = (to_core, to_x, to_up, to_down, to_right, to_left, to_far, to_next, to_prev)

    barrier = pltpu.get_barrier_semaphore()
    for partner in partners:
        pl.semaphore_signal(barrier, inc=1, device_id=partner, device_id_type=MESH)

    copies = []

    def send(source, target, device):
        index = len(copies)
        copy = pltpu.make_async_remote_copy(
            src_ref=source,
            dst_ref=target,
            send_sem=send_sem.at[index],
            recv_sem=recv_sem.at[index],
            device_id=device,
            device_id_type=MESH,
        )
        copy.start()
        copies.append(copy)
        return copy

    atom_lane = lax.broadcasted_iota(jnp.int32, (2 * GHOSTS, ATOMS), 1)
    pick = (atom_lane == ghost_col[...]).astype(BF16)
    ghosts = jnp.dot(pick, features[...], preferred_element_type=F32)
    for side in range(2):
        mine = ghosts[side * GHOSTS : (side + 1) * GHOSTS]
        ghost_send[side] = jnp.concatenate([mine[:, :PACK], mine[:, WIDTH - PACK :]], 0).astype(BF16)

    pl.semaphore_wait(barrier, len(partners))

    ghost_copies = [
        send(ghost_send.at[0], ghost_recv.at[0], to_next),
        send(ghost_send.at[1], ghost_recv.at[1], to_prev),
    ]
    raw_x, raw_core, raw_xc = {}, {}, {}
    for k in range(3):
        raw_x[k] = send(w[k], raw[k].at[1], to_x)
        raw_core[k] = send(w[k], raw[k].at[0], to_core)

    def forward_raw(k):
        raw_x[k].wait_recv()
        raw_xc[k] = send(raw[k].at[1], raw[k].at[2], to_core)

    z_first, z_direct, z_sum = {}, {}, {}

    def partials(k):
        raw_core[k].wait_recv()
        raw_xc[k].wait_recv()
        across = COLS[k] // 128
        scale = [
            [
                mixture[(xl * 4 + (z + step) % 4) * 2 + core, 2 * owner + i]
                for owner in (dp, dp_core, dp_x, dp_xc)
                for i in range(2)
            ]
            for step in range(4)
        ]
        for mat in range(MATS[k]):
            lead = () if k == 0 else (mat,)

            def body(t, mat=mat, lead=lead):
                rs = tiles16(t // across)
                c = pl.ds(pl.multiple_of((t % across) * 128, 128), 128)
                terms = [w[k][(i,) + lead + (rs, c)].astype(F32) for i in range(2)]
                for slot in range(3):
                    terms += [raw[k][(slot, i) + lead + (rs, c)].astype(F32) for i in range(2)]
                for step in range(4):
                    total = scale[step][0] * terms[0]
                    for factor, term in zip(scale[step][1:], terms[1:]):
                        total = total + factor * term
                    par[k][lead + (step, rs, c)] = total.astype(BF16)

            steps(ROWS[k] // 16 * across, body)
        for h, half in enumerate(HALVES):
            if half[0] != k:
                continue
            if half[4]:
                z_first[h] = send(part(par[k], half, (2,)), part(zf[k], half, ()), to_up)
                z_direct[h] = send(part(par[k], half, (3,)), part(zr[k], half, ()), to_down)
            else:
                z_first[h] = send(part(par[k], half, (2,)), part(zf[k], half, ()), to_down)
                z_direct[h] = send(part(par[k], half, (1,)), part(zl[k], half, ()), to_up)

    def add_into(target, extra, rows):
        def body(i):
            rs = tiles16(i)
            target[rs] = (target[rs].astype(F32) + extra[rs].astype(F32)).astype(BF16)

        steps(rows // 16, body)

    def relay_sums(k):
        for h, half in enumerate(HALVES):
            if half[0] != k:
                continue
            step = 1 if half[4] else 3
            z_first[h].wait_recv()
            add_into(part(par[k], half, (step,)), part(zf[k], half, ()), half[3])
            target = zl[k] if half[4] else zr[k]
            z_sum[h] = send(
                part(par[k], half, (step,)), part(target, half, ()), to_up if half[4] else to_down
            )

    b_far, b_right, b_left, b_relay = {}, {}, {}, {}

    def spread(k, own):
        place = xh if own else 1 - xh
        here = whole(mix[k], k, (place, y))
        b_right[k, own] = send(here, here, to_right)
        b_left[k, own] = send(here, here, to_left)

    def finish_mix(k):
        for h, half in enumerate(HALVES):
            if half[0] != k:
                continue
            z_direct[h].wait_recv()
            z_sum[h].wait_recv()
            own, up, down = (
                part(par[k], half, (0,)),
                part(zl[k], half, ()),
                part(zr[k], half, ()),
            )
            target = part(mix[k], half, (xh, y))

            def body(i, own=own, up=up, down=down, target=target):
                rs = tiles16(i)
                total = own[rs].astype(F32) + up[rs].astype(F32) + down[rs].astype(F32)
                target[rs] = total.astype(BF16)

            steps(half[3] // 16, body)
        here = whole(mix[k], k, (xh, y))
        b_far[k] = send(here, here, to_far)
        spread(k, True)

    xo = 1 - xh

    def spread_far(k):
        b_far[k].wait_recv()
        spread(k, False)

    def relay_mix(k, own):
        place = xh if own else xo
        b_right[k, own].wait_recv()
        b_left[k, own].wait_recv()
        for h, half in enumerate(HALVES):
            if half[0] != k:
                continue
            step = 3 if half[4] else 1
            here = part(mix[k], half, (place, (y + step) % 4))
            b_relay[h, own] = send(here, here, to_right if half[4] else to_left)

    c_first, c_direct, c_sum, c_far = {}, {}, {}, {}

    def weight_grads(k):
        rows = ROWS[k]
        for place in range(2):

            def body(b, place=place):
                rs = pl.ds(pl.multiple_of((place * 4 + b) * rows, 16), rows)
                if k == 0:
                    total = contract(v0[rs], d0[...], 1, 1)
                    gw0[place, b] = (WEIGHT_SCALE * total).astype(BF16)
                else:
                    left, right, swapped = ((v1, d1, s1), (v2, d2, s2))[k - 1]
                    left = left[rs]
                    real = contract(left, right[...], 1, 1)
                    gw[k][0, place, b] = (WEIGHT_SCALE * real).astype(BF16)
                    imag = contract(left, swapped[...], 1, 1)
                    gw[k][1, place, b] = (WEIGHT_SCALE * imag).astype(BF16)

            steps(4, body)
        for h, half in enumerate(HALVES):
            if half[0] != k:
                continue
            chunk, mat, first, rows, up = half

            def both(ref, step=None):
                lead = (slice(None),) if step is None else (slice(None), (y + step) % 4)
                if k == 0:
                    return ref.at[lead + (pl.ds(first, rows),)]
                return ref.at[(mat,) + lead]

            if up:
                c_first[h] = send(both(gw[k], 2), both(cf[k]), to_right)
                c_direct[h] = send(both(gw[k], 3), both(cr[k]), to_left)
            else:
                c_first[h] = send(both(gw[k], 2), both(cf[k]), to_left)
                c_direct[h] = send(both(gw[k], 1), both(cl[k]), to_right)

    def relay_grads(k):
        for h, half in enumerate(HALVES):
            if half[0] != k:
                continue
            chunk, mat, first, rows, up = half
            step = 1 if up else 3
            c_first[h].wait_recv()
            for place in range(2):
                add_into(
                    part(gw[k], half, (place, (y + step) % 4)), part(cf[k], half, (place,)), rows
                )
            target = cl[k] if up else cr[k]
            if k == 0:
                source = gw[k].at[:, (y + step) % 4, pl.ds(first, rows)]
                target = target.at[:, pl.ds(first, rows)]
            else:
                source = gw[k].at[mat, :, (y + step) % 4]
                target = target.at[mat]
            c_sum[h] = send(source, target, to_right if up else to_left)

    def halves_of(k, body):
        for half in HALVES:
            if half[0] == k:
                body(half)

    def sum_grads(k):
        for h, half in enumerate(HALVES):
            if half[0] == k:
                c_direct[h].wait_recv()
                c_sum[h].wait_recv()

        def one(half):
            terms = (
                part(gw[k], half, (xo, y)),
                part(cl[k], half, (xo,)),
                part(cr[k], half, (xo,)),
            )
            target = part(cs[k], half, ())

            def body(i):
                rs = tiles16(i)
                total = terms[0][rs].astype(F32) + terms[1][rs].astype(F32) + terms[2][rs].astype(F32)
                target[rs] = total.astype(BF16)

            steps(half[3] // 16, body)

        halves_of(k, one)
        c_far[k] = send(cs[k], cx[k], to_far)

    def finish_grads(k):
        c_far[k].wait_recv()

        def one(half):
            terms = (
                part(gw[k], half, (xh, y)),
                part(cl[k], half, (xh,)),
                part(cr[k], half, (xh,)),
                part(cx[k], half, ()),
            )
            target = part(out[k], half, (0,)) if k == 0 else out[k].at[0, half[1]]

            def body(i):
                rs = tiles16(i)
                total = terms[0][rs].astype(F32) + terms[1][rs].astype(F32)
                total = total + terms[2][rs].astype(F32) + terms[3][rs].astype(F32)
                target[rs] = total.astype(BF16)

            steps(half[3] // 16, body)

        halves_of(k, one)

    wig32[0:WIG] = wigner[...].astype(F32)
    for degree in range(LMAX + 1):
        extent, kept = 2 * degree + 1, min(degree, MMAX)
        start = degree * (2 * degree - 1) * (2 * degree + 1) // 3 + (degree - kept) * extent
        for j in range(2 * kept + 1):
            rows = wig32[start + j * extent : start + (j + 1) * extent]
            blocks[degree][j] = jnp.broadcast_to(rows[:, None, :], (extent, 8, EDGES))

    live = lax.broadcasted_iota(jnp.int32, (ATOMS, EDGES), 1) < count[0, 0]
    hot_target = (
        (lax.broadcasted_iota(jnp.int32, (ATOMS, EDGES), 0) == targets[...]) & live
    ).astype(F32)
    hot_quarter = (MESSAGE_SCALE * hot_target).astype(BF16)
    hot_target = hot_target.astype(BF16)
    hot_source = (
        lax.broadcasted_iota(jnp.int32, (ATOMS + 2 * GHOSTS, EDGES), 0) == sources[...]
    ).astype(BF16)

    def wide(i):
        return pl.ds(pl.multiple_of(i * 896, 128), 896)

    def back_gather(i):
        rows_b[wide(i)] = contract(grad_out[:, wide(i)], hot_quarter, 0, 0).astype(BF16)

    steps(7, back_gather)

    for copy in ghost_copies:
        copy.wait_recv()
    table[0:ATOMS] = features[...]
    came = [ghost_recv[side].astype(F32) for side in range(2)]
    for low, high, first, cut in ((0, PACK, 0, 0), (PACK, WIDTH, GHOSTS, 2 * PACK - WIDTH)):
        both = [a[first : first + GHOSTS, cut : cut + high - low] for a in came]
        table[ATOMS : ATOMS + 2 * GHOSTS, low:high] = jnp.concatenate(both, 0).astype(BF16)

    def gather(i):
        rows_f[wide(i)] = contract(table[:, wide(i)], hot_source, 0, 0).astype(BF16)

    steps(7, gather)

    def rotate_into(i):
        for source, f0, f1, f2 in ((rows_f, v0, v1, v2), (rows_b, d0, d1, d2)):
            for degree in range(LMAX + 1):
                kept = min(degree, MMAX)
                total = None
                for n in range(2 * degree + 1):
                    first = (degree * degree + n) * 128
                    row = source[pl.ds(pl.multiple_of(first + i * 16, 16), 16)].astype(F32)
                    factor = blocks[degree][:, n]
                    term = factor[:, None] * row.reshape(1, 2, 8, EDGES)
                    total = term if total is None else total + term
                result = total.reshape(2 * kept + 1, 16, EDGES).astype(BF16)
                f0[pl.ds(pl.multiple_of(degree * 128 + i * 16, 16), 16)] = result[kept]
                for order, target in ((1, f1), (2, f2)):
                    if kept >= order:
                        rs = pl.ds(pl.multiple_of((degree - order) * 128 + i * 16, 16), 16)
                        target[rs, 0:EDGES] = result[kept + order]
                        target[rs, EDGES : 2 * EDGES] = result[kept - order]

    steps(8, rotate_into)

    for source, target in ((d1, s1), (d2, s2)):
        target[:, 0:EDGES] = source[:, EDGES : 2 * EDGES]
        target[:, EDGES : 2 * EDGES] = -source[:, 0:EDGES]
    t0[...] = v0[...].T
    for source, target, swapped in ((v1, t1, u1), (v2, t2, u2)):
        target[...] = source[...].T
        swapped[0:EDGES] = -target[EDGES : 2 * EDGES]
        swapped[EDGES : 2 * EDGES] = target[0:EDGES]

    forward_raw(0)
    partials(0)
    weight_grads(0)
    relay_sums(0)
    weight_grads(2)
    finish_mix(0)
    forward_raw(1)
    partials(1)
    spread_far(0)
    relay_mix(0, True)
    weight_grads(1)
    relay_sums(1)
    relay_mix(0, False)
    finish_mix(1)
    forward_raw(2)
    partials(2)
    spread_far(1)
    relay_grads(0)
    relay_sums(2)
    relay_mix(1, True)
    finish_mix(2)
    relay_mix(1, False)
    relay_grads(2)
    spread_far(2)
    relay_mix(2, True)
    relay_grads(1)
    relay_mix(2, False)
    sum_grads(0)

    def convolve(k):
        for h, half in enumerate(HALVES):
            if half[0] == k:
                b_relay[h, True].wait_recv()
                b_relay[h, False].wait_recv()
        width = COLS[k]
        if k == 0:
            weight = mix0[...].reshape(width, width)
            v0[...] = jnp.dot(t0[...], weight, preferred_element_type=F32).T.astype(BF16)
            d0[...] = jnp.dot(weight, d0[...], preferred_element_type=F32).astype(BF16)
            return
        t, u, v, d, s = ((t1, u1, v1, d1, s1), (t2, u2, v2, d2, s2))[k - 1]
        real = mix[k][0].reshape(width, width)
        imag = mix[k][1].reshape(width, width)
        result = jnp.dot(t[...], real, preferred_element_type=F32)
        result = result + jnp.dot(u[...], imag, preferred_element_type=F32)
        v[...] = result.T.astype(BF16)
        result = jnp.dot(real, d[...], preferred_element_type=F32)
        d[...] = (result + jnp.dot(imag, s[...], preferred_element_type=F32)).astype(BF16)

    convolve(0)
    sum_grads(2)
    convolve(1)
    sum_grads(1)
    convolve(2)

    def rotate_back(target, f0, f1, f2):
        def body(i):
            for degree in range(LMAX + 1):
                extent, kept = 2 * degree + 1, min(degree, MMAX)
                rows = []
                for order in range(-kept, kept + 1):
                    source = (f0, f1, f2)[abs(order)]
                    rs = pl.ds(pl.multiple_of((degree - abs(order)) * 128 + i * 16, 16), 16)
                    lanes = slice(EDGES, 2 * EDGES) if order < 0 else slice(0, EDGES)
                    rows.append(source[rs, lanes].astype(F32).reshape(2, 8, EDGES))
                for n in range(extent):
                    total = None
                    for j, row in enumerate(rows):
                        term = blocks[degree][j, n][None] * row
                        total = term if total is None else total + term
                    first = (degree * degree + n) * 128
                    target[pl.ds(pl.multiple_of(first + i * 16, 16), 16)] = total.reshape(
                        16, EDGES
                    ).astype(BF16)

        steps(8, body)

    rotate_back(rows_b, d0, d1, d2)

    def scatter_back(i):
        total = contract(hot_source, rows_b[wide(i)], 1, 1)
        table_own[:, wide(i)] = total[0:ATOMS]
        table_ghost[:, wide(i)] = total[ATOMS : ATOMS + 2 * GHOSTS]

    steps(7, scatter_back)
    for side in range(2):
        mine = table_ghost[side * GHOSTS : (side + 1) * GHOSTS]
        back_send[side] = jnp.concatenate([mine[:, :PACK], mine[:, WIDTH - PACK :]], 0).astype(BF16)
    back_copies = [
        send(back_send.at[0], back_recv.at[0], to_prev),
        send(back_send.at[1], back_recv.at[1], to_next),
    ]

    rotate_back(rows_f, v0, v1, v2)

    def scatter(i):
        total = contract(hot_target, rows_f[wide(i)], 1, 1)
        updated[:, wide(i)] = (
            features[:, wide(i)].astype(F32) + MESSAGE_SCALE * total
        ).astype(BF16)

    steps(7, scatter)

    for k in (0, 2, 1):
        finish_grads(k)

    for copy in back_copies:
        copy.wait_recv()
    came = [back_recv[side].astype(F32) for side in range(2)]
    spots = (
        lax.broadcasted_iota(jnp.int32, (ATOMS, 2 * GHOSTS), 0) == ghost_row[...]
    ).astype(BF16)
    for low, high, first, cut in ((0, PACK, 0, 0), (PACK, WIDTH, GHOSTS, 2 * PACK - WIDTH)):
        both = [a[first : first + GHOSTS, cut : cut + high - low] for a in came]
        both = jnp.concatenate(both, 0).astype(BF16)
        total = grad_out[:, low:high].astype(F32) + table_own[:, low:high]
        total = total + jnp.dot(spots, both, preferred_element_type=F32)
        grad_features[:, low:high] = total.astype(BF16)

    for copy in copies:
        copy.wait_send()


def on_device(
    features, grad_out, wigner, sources, targets, ghost_index, edge_count, mixture,
    w_zero, w_one, w_two,
):
    def buffers(*lead):
        shapes = []
        for k in range(3):
            mats = () if k == 0 else (2,)
            shapes.append(pltpu.VMEM(mats + lead + (ROWS[k], COLS[k]), BF16))
        return shapes

    raw = [
        pltpu.VMEM((3, 2) + (() if k == 0 else (2,)) + (ROWS[k], COLS[k]), BF16) for k in range(3)
    ]
    frame = [
        pltpu.VMEM((896, EDGES), BF16),
        pltpu.VMEM((768, 2 * EDGES), BF16),
        pltpu.VMEM((640, 2 * EDGES), BF16),
    ]
    turned = [
        pltpu.VMEM((EDGES, 896), BF16),
        pltpu.VMEM((2 * EDGES, 768), BF16),
        pltpu.VMEM((2 * EDGES, 640), BF16),
    ]
    exchange = [pltpu.VMEM((2, 2 * GHOSTS, PACK), BF16)] * 4
    scratch = (
        raw
        + buffers(4)
        + buffers() * 3
        + buffers(2, 4)
        + buffers(2, 4)
        + buffers(2) * 3
        + buffers() * 2
        + exchange
        + [pltpu.VMEM((456, EDGES), F32)]
        + [
            pltpu.VMEM((2 * min(degree, MMAX) + 1, 2 * degree + 1, 8, EDGES), F32)
            for degree in range(LMAX + 1)
        ]
        + [pltpu.VMEM((ATOMS + 2 * GHOSTS, WIDTH), BF16)]
        + [pltpu.VMEM((WIDTH, EDGES), BF16)] * 2
        + frame * 2
        + frame[1:]
        + turned
        + turned[1:]
        + [pltpu.VMEM((ATOMS, WIDTH), F32), pltpu.VMEM((2 * GHOSTS, WIDTH), F32)]
        + [pltpu.SemaphoreType.DMA((COPIES,))] * 2
    )
    vmem = pl.BlockSpec(memory_space=pltpu.VMEM)
    smem = pl.BlockSpec(memory_space=pltpu.SMEM)
    return pl.pallas_call(
        kernel,
        out_shape=(
            jax.ShapeDtypeStruct((ATOMS, WIDTH), BF16),
            jax.ShapeDtypeStruct((ATOMS, WIDTH), BF16),
            jax.ShapeDtypeStruct((1, 112, 896), BF16),
            jax.ShapeDtypeStruct((1, 2, 96, 768), BF16),
            jax.ShapeDtypeStruct((1, 2, 80, 640), BF16),
        ),
        in_specs=[smem, smem] + [vmem] * 10,
        out_specs=(vmem,) * 5,
        scratch_shapes=scratch,
        compiler_params=pltpu.CompilerParams(
            collective_id=0, has_side_effects=True, vmem_limit_bytes=58 * 1024 * 1024
        ),
        name="message_layer",
    )(
        mixture,
        edge_count,
        features,
        grad_out,
        wigner,
        sources.reshape(1, -1),
        targets.reshape(1, -1),
        ghost_index.reshape(-1, 1),
        ghost_index.reshape(1, -1),
        w_zero,
        w_one,
        w_two,
    )


def solution(mesh):
    both = ("dp", "space")
    return jax.shard_map(
        on_device,
        mesh=mesh,
        in_specs=(
            P(both, None),
            P(both, None),
            P(None, both),
            P(both),
            P(both),
            P(both, None, None),
            P("dp", "space"),
            P(),
            P("dp", "space", None),
            P("dp", None, "space", None),
            P("dp", None, "space", None),
        ),
        out_specs=(
            P(both, None),
            P(both, None),
            P("dp", "space", None),
            P("dp", None, "space", None),
            P("dp", None, "space", None),
        ),
        check_vma=False,
    )
```

```python
import functools

import jax
import jax.numpy as jnp
from jax import lax
from jax.experimental import pallas as pl
from jax.experimental.pallas import tpu as pltpu
from jax.sharding import PartitionSpec as P

BF16 = jnp.bfloat16
F32 = jnp.float32
MESH = pl.DeviceIdType.MESH

LMAX = 6
MMAX = 2
EDGES = 128
ATOMS = 32
GHOSTS = 8
WIDTH = 6272
PACK = 3200
WIG_READ = 416
MESSAGE_SCALE = 0.25
WEIGHT_SCALE = 1024.0 ** -0.5

ROWS = (112, 96, 80)
COLS = (896, 768, 640)
MATS = (1, 2, 2)
HALVES = (
    (0, 0, 0, 48, True),
    (0, 0, 48, 64, False),
    (1, 0, 0, 96, True),
    (1, 1, 0, 96, False),
    (2, 0, 0, 80, True),
    (2, 1, 0, 80, False),
)
COPIES = 128


def contract(left, right, left_dim, right_dim):
    return lax.dot_general(
        left, right, (((left_dim,), (right_dim,)), ((), ())), preferred_element_type=F32
    )


def whole(ref, chunk, lead):
    return ref.at[lead] if chunk == 0 else ref.at[(slice(None),) + lead]


def part(ref, half, lead):
    chunk, mat, first, rows, _ = half
    if chunk == 0:
        return ref.at[lead + (pl.ds(first, rows),)]
    return ref.at[(mat,) + lead]


def steps(count, body):
    def step(i, carry):
        body(i)
        return carry

    lax.fori_loop(0, count, step, 0)


def tiles16(i):
    return pl.ds(pl.multiple_of(i * 16, 16), 16)


def kernel(
    mixture, count, features, grad_out, wigner, sources, targets, ghost_col, ghost_row, w0, w1, w2,
    updated, grad_features, out0, out1, out2,
    raw0, raw1, raw2, par0, par1, par2, zf0, zf1, zf2, zl0, zl1, zl2, zr0, zr1, zr2,
    mix0, mix1, mix2, gw0, gw1, gw2, cf0, cf1, cf2, cl0, cl1, cl2, cr0, cr1, cr2,
    far_grad, far_wigner, hot_send, far_hot, far_v0, far_v1, far_v2,
    ghost_send, ghost_recv, back_send, back_recv,
    wig32, blk0, blk1, blk2, blk3, blk4, blk5, blk6, fbk0, fbk1, fbk2, fbk3, fbk4, fbk5, fbk6,
    table, rows_f, rows_b, rows_p, v0, v1, v2, d0, d1, d2, p0, p1, p2, s1, s2, q1, q2, t0, t1, t2, u1, u2,
    table_own, table_ghost, send_sem, recv_sem,
):
    w = (w0, w1, w2)
    raw = (raw0, raw1, raw2)
    par = (par0, par1, par2)
    zf, zl, zr = (zf0, zf1, zf2), (zl0, zl1, zl2), (zr0, zr1, zr2)
    mix = (mix0, mix1, mix2)
    gw = (gw0, gw1, gw2)
    cf, cl, cr = (cf0, cf1, cf2), (cl0, cl1, cl2), (cr0, cr1, cr2)
    far_v = (far_v0, far_v1, far_v2)
    out = (out0, out1, out2)
    blocks = (blk0, blk1, blk2, blk3, blk4, blk5, blk6)
    far_blocks = (fbk0, fbk1, fbk2, fbk3, fbk4, fbk5, fbk6)

    dp, sp = lax.axis_index("dp"), lax.axis_index("space")
    core, z, xl = dp % 2, (dp // 2) % 4, dp // 8
    y, xh = sp % 4, sp // 4
    dp_core = dp + 1 - 2 * core
    dp_x = (1 - xl) * 8 + z * 2 + core
    dp_xc = (1 - xl) * 8 + z * 2 + 1 - core
    sp_x = (1 - xh) * 4 + y

    def at_z(step):
        return xl * 8 + ((z + step) % 4) * 2 + core

    def at_y(step):
        return xh * 4 + (y + step) % 4

    to_core, to_x = (dp_core, sp), (dp_x, sp)
    to_up, to_down = (at_z(1), sp), (at_z(3), sp)
    to_right, to_left = (dp, at_y(1)), (dp, at_y(3))
    to_far = (dp, sp_x)
    to_next, to_prev = (dp, (sp + 1) % 8), (dp, (sp + 7) % 8)
    partners = (to_core, to_x, to_up, to_down, to_right, to_left, to_far, to_next, to_prev)

    barrier = pltpu.get_barrier_semaphore()
    for partner in partners:
        pl.semaphore_signal(barrier, inc=1, device_id=partner, device_id_type=MESH)

    copies = []

    def send(source, target, device):
        index = len(copies)
        copy = pltpu.make_async_remote_copy(
            src_ref=source,
            dst_ref=target,
            send_sem=send_sem.at[index],
            recv_sem=recv_sem.at[index],
            device_id=device,
            device_id_type=MESH,
        )
        copy.start()
        copies.append(copy)
        return copy

    atom_lane = lax.broadcasted_iota(jnp.int32, (2 * GHOSTS, ATOMS), 1)
    pick = (atom_lane == ghost_col[...]).astype(BF16)
    ghosts = jnp.dot(pick, features[...], preferred_element_type=F32)
    for side in range(2):
        mine = ghosts[side * GHOSTS : (side + 1) * GHOSTS]
        ghost_send[side] = jnp.concatenate([mine[:, :PACK], mine[:, WIDTH - PACK :]], 0).astype(BF16)

    live = lax.broadcasted_iota(jnp.int32, (ATOMS, EDGES), 1) < count[0, 0]
    hot_target = (
        (lax.broadcasted_iota(jnp.int32, (ATOMS, EDGES), 0) == targets[...]) & live
    ).astype(F32)
    hot_quarter = (MESSAGE_SCALE * hot_target).astype(BF16)
    hot_target = hot_target.astype(BF16)
    hot_source = (
        lax.broadcasted_iota(jnp.int32, (ATOMS + 2 * GHOSTS, EDGES), 0) == sources[...]
    ).astype(BF16)

    hot_send[...] = hot_quarter

    pl.semaphore_wait(barrier, len(partners))

    ghost_copies = [
        send(ghost_send.at[0], ghost_recv.at[0], to_next),
        send(ghost_send.at[1], ghost_recv.at[1], to_prev),
    ]
    raw_x, raw_core, raw_xc = {}, {}, {}
    far_copies = []
    for k in range(3):
        raw_x[k] = send(w[k], raw[k].at[1], to_x)
        raw_core[k] = send(w[k], raw[k].at[0], to_core)
        if k == 0:
            far_copies.append(send(grad_out, far_grad, to_far))
            far_copies.append(send(wigner.at[0:WIG_READ], far_wigner, to_far))
            far_copies.append(send(hot_send, far_hot, to_far))

    def forward_raw(k):
        raw_x[k].wait_recv()
        raw_xc[k] = send(raw[k].at[1], raw[k].at[2], to_core)

    z_first, z_direct, z_sum = {}, {}, {}

    def partials(k):
        raw_core[k].wait_recv()
        raw_xc[k].wait_recv()
        across = COLS[k] // 128
        scale = [
            [
                mixture[(xl * 4 + (z + step) % 4) * 2 + core, 2 * owner + i]
                for owner in (dp, dp_core, dp_x, dp_xc)
                for i in range(2)
            ]
            for step in range(4)
        ]
        for mat in range(MATS[k]):
            lead = () if k == 0 else (mat,)

            def body(t, mat=mat, lead=lead):
                rs = tiles16(t // across)
                c = pl.ds(pl.multiple_of((t % across) * 128, 128), 128)
                terms = [w[k][(i,) + lead + (rs, c)].astype(F32) for i in range(2)]
                for slot in range(3):
                    terms += [raw[k][(slot, i) + lead + (rs, c)].astype(F32) for i in range(2)]
                for step in range(4):
                    total = scale[step][0] * terms[0]
                    for factor, term in zip(scale[step][1:], terms[1:]):
                        total = total + factor * term
                    par[k][lead + (step, rs, c)] = total.astype(BF16)

            steps(ROWS[k] // 16 * across, body)
        for h, half in enumerate(HALVES):
            if half[0] != k:
                continue
            if half[4]:
                z_first[h] = send(part(par[k], half, (2,)), part(zf[k], half, ()), to_up)
                z_direct[h] = send(part(par[k], half, (3,)), part(zr[k], half, ()), to_down)
            else:
                z_first[h] = send(part(par[k], half, (2,)), part(zf[k], half, ()), to_down)
                z_direct[h] = send(part(par[k], half, (1,)), part(zl[k], half, ()), to_up)

    def add_into(target, extra, rows):
        def body(i):
            rs = tiles16(i)
            target[rs] = (target[rs].astype(F32) + extra[rs].astype(F32)).astype(BF16)

        steps(rows // 16, body)

    def relay_sums(k):
        for h, half in enumerate(HALVES):
            if half[0] != k:
                continue
            step = 1 if half[4] else 3
            z_first[h].wait_recv()
            add_into(part(par[k], half, (step,)), part(zf[k], half, ()), half[3])
            target = zl[k] if half[4] else zr[k]
            z_sum[h] = send(
                part(par[k], half, (step,)), part(target, half, ()), to_up if half[4] else to_down
            )

    b_far, b_right, b_left, b_relay = {}, {}, {}, {}

    def spread(k, own):
        place = xh if own else 1 - xh
        here = whole(mix[k], k, (place, y))
        b_right[k, own] = send(here, here, to_right)
        b_left[k, own] = send(here, here, to_left)

    def finish_mix(k):
        for h, half in enumerate(HALVES):
            if half[0] != k:
                continue
            z_direct[h].wait_recv()
            z_sum[h].wait_recv()
            own, up, down = (
                part(par[k], half, (0,)),
                part(zl[k], half, ()),
                part(zr[k], half, ()),
            )
            target = part(mix[k], half, (xh, y))

            def body(i, own=own, up=up, down=down, target=target):
                rs = tiles16(i)
                total = own[rs].astype(F32) + up[rs].astype(F32) + down[rs].astype(F32)
                target[rs] = total.astype(BF16)

            steps(half[3] // 16, body)
        here = whole(mix[k], k, (xh, y))
        b_far[k] = send(here, here, to_far)
        spread(k, True)

    xo = 1 - xh

    def spread_far(k):
        b_far[k].wait_recv()
        spread(k, False)

    def relay_mix(k, own):
        place = xh if own else xo
        b_right[k, own].wait_recv()
        b_left[k, own].wait_recv()
        for h, half in enumerate(HALVES):
            if half[0] != k:
                continue
            step = 3 if half[4] else 1
            here = part(mix[k], half, (place, (y + step) % 4))
            b_relay[h, own] = send(here, here, to_right if half[4] else to_left)

    c_first, c_direct, c_sum = {}, {}, {}

    def weight_grads(k):
        rows = ROWS[k]
        far_rows[k].wait_recv()

        def body(b):
            own = pl.ds(pl.multiple_of((xh * 4 + b) * rows, 16), rows)
            far = pl.ds(pl.multiple_of(b * rows, 16), rows)
            if k == 0:
                total = contract(v0[own], d0[...], 1, 1) + contract(far_v0[far], p0[...], 1, 1)
                gw0[b] = (WEIGHT_SCALE * total).astype(BF16)
            else:
                v, d, s, p, q = ((v1, d1, s1, p1, q1), (v2, d2, s2, p2, q2))[k - 1]
                mine, other = v[own], far_v[k][far]
                real = contract(mine, d[...], 1, 1) + contract(other, p[...], 1, 1)
                gw[k][0, b] = (WEIGHT_SCALE * real).astype(BF16)
                imag = contract(mine, s[...], 1, 1) + contract(other, q[...], 1, 1)
                gw[k][1, b] = (WEIGHT_SCALE * imag).astype(BF16)

        steps(4, body)
        for h, half in enumerate(HALVES):
            if half[0] != k:
                continue

            def block(step, half=half):
                return part(gw[k], half, ((y + step) % 4,))

            if half[4]:
                c_first[h] = send(block(2), part(cf[k], half, ()), to_right)
                c_direct[h] = send(block(3), part(cr[k], half, ()), to_left)
            else:
                c_first[h] = send(block(2), part(cf[k], half, ()), to_left)
                c_direct[h] = send(block(1), part(cl[k], half, ()), to_right)

    def relay_grads(k):
        for h, half in enumerate(HALVES):
            if half[0] != k:
                continue
            here = part(gw[k], half, ((y + (1 if half[4] else 3)) % 4,))
            c_first[h].wait_recv()
            add_into(here, part(cf[k], half, ()), half[3])
            target = cl[k] if half[4] else cr[k]
            c_sum[h] = send(here, part(target, half, ()), to_right if half[4] else to_left)

    def finish_grads(k):
        for h, half in enumerate(HALVES):
            if half[0] != k:
                continue
            c_direct[h].wait_recv()
            c_sum[h].wait_recv()
            own, left, right = (
                part(gw[k], half, (y,)),
                part(cl[k], half, ()),
                part(cr[k], half, ()),
            )
            target = part(out[k], half, (0,)) if k == 0 else out[k].at[0, half[1]]

            def body(i, own=own, left=left, right=right, target=target):
                rs = tiles16(i)
                total = own[rs].astype(F32) + left[rs].astype(F32) + right[rs].astype(F32)
                target[rs] = total.astype(BF16)

            steps(half[3] // 16, body)

    def expand(matrix, target):
        wig32[...] = matrix[0:WIG_READ].astype(F32)
        for degree in range(LMAX + 1):
            extent, kept = 2 * degree + 1, min(degree, MMAX)
            start = degree * (2 * degree - 1) * (2 * degree + 1) // 3 + (degree - kept) * extent
            for j in range(2 * kept + 1):
                rows = wig32[start + j * extent : start + (j + 1) * extent]
                target[degree][j] = jnp.broadcast_to(rows[:, None, :], (extent, 8, EDGES))

    expand(wigner, blocks)

    def wide(i):
        return pl.ds(pl.multiple_of(i * 896, 128), 896)

    def back_gather(i):
        rows_b[wide(i)] = contract(grad_out[:, wide(i)], hot_quarter, 0, 0).astype(BF16)

    steps(7, back_gather)

    for copy in ghost_copies:
        copy.wait_recv()
    table[0:ATOMS] = features[...]
    came = [ghost_recv[side].astype(F32) for side in range(2)]
    for low, high, first, cut in ((0, PACK, 0, 0), (PACK, WIDTH, GHOSTS, 2 * PACK - WIDTH)):
        both = [a[first : first + GHOSTS, cut : cut + high - low] for a in came]
        table[ATOMS : ATOMS + 2 * GHOSTS, low:high] = jnp.concatenate(both, 0).astype(BF16)

    def gather(i):
        rows_f[wide(i)] = contract(table[:, wide(i)], hot_source, 0, 0).astype(BF16)

    steps(7, gather)

    def rotate_into(i, frames, matrices):
        for source, f0, f1, f2 in frames:
            for degree in range(LMAX + 1):
                kept = min(degree, MMAX)
                total = None
                for n in range(2 * degree + 1):
                    first = (degree * degree + n) * 128
                    row = source[pl.ds(pl.multiple_of(first + i * 16, 16), 16)].astype(F32)
                    factor = matrices[degree][:, n]
                    term = factor[:, None] * row.reshape(1, 2, 8, EDGES)
                    total = term if total is None else total + term
                result = total.reshape(2 * kept + 1, 16, EDGES).astype(BF16)
                f0[pl.ds(pl.multiple_of(degree * 128 + i * 16, 16), 16)] = result[kept]
                for order, target in ((1, f1), (2, f2)):
                    if kept >= order:
                        rs = pl.ds(pl.multiple_of((degree - order) * 128 + i * 16, 16), 16)
                        target[rs, 0:EDGES] = result[kept + order]
                        target[rs, EDGES : 2 * EDGES] = result[kept - order]

    steps(8, lambda i: rotate_into(i, ((rows_f, v0, v1, v2), (rows_b, d0, d1, d2)), blocks))
    far_rows = []
    for k, source in enumerate((v0, v1, v2)):
        rows = 4 * ROWS[k]
        half = source.at[pl.ds(pl.multiple_of((1 - xh) * rows, 16), rows)]
        far_rows.append(send(half, far_v[k], to_far))

    def swap(source, target):
        target[:, 0:EDGES] = source[:, EDGES : 2 * EDGES]
        target[:, EDGES : 2 * EDGES] = -source[:, 0:EDGES]

    swap(d1, s1)
    swap(d2, s2)
    t0[...] = v0[...].T
    for source, target, swapped in ((v1, t1, u1), (v2, t2, u2)):
        target[...] = source[...].T
        swapped[0:EDGES] = -target[EDGES : 2 * EDGES]
        swapped[EDGES : 2 * EDGES] = target[0:EDGES]

    def far_frame():
        for copy in far_copies:
            copy.wait_recv()
        expand(far_wigner, far_blocks)
        hot = far_hot[...]

        def far_gather(i):
            rows_p[wide(i)] = contract(far_grad[:, wide(i)], hot, 0, 0).astype(BF16)

        steps(7, far_gather)
        steps(8, lambda i: rotate_into(i, ((rows_p, p0, p1, p2),), far_blocks))
        swap(p1, q1)
        swap(p2, q2)

    forward_raw(0)
    partials(0)
    far_frame()
    relay_sums(0)
    finish_mix(0)
    forward_raw(1)
    weight_grads(0)
    partials(1)
    spread_far(0)
    relay_mix(0, True)
    relay_sums(1)
    relay_mix(0, False)
    finish_mix(1)
    forward_raw(2)
    weight_grads(1)
    partials(2)
    spread_far(1)
    relay_grads(0)
    relay_sums(2)
    relay_mix(1, True)
    finish_mix(2)
    weight_grads(2)
    relay_mix(1, False)
    spread_far(2)
    relay_mix(2, True)
    relay_grads(1)
    relay_mix(2, False)
    relay_grads(2)

    def convolve(k):
        for h, half in enumerate(HALVES):
            if half[0] == k:
                b_relay[h, True].wait_recv()
                b_relay[h, False].wait_recv()
        width = COLS[k]
        if k == 0:
            weight = mix0[...].reshape(width, width)
            v0[...] = jnp.dot(t0[...], weight, preferred_element_type=F32).T.astype(BF16)
            d0[...] = jnp.dot(weight, d0[...], preferred_element_type=F32).astype(BF16)
            return
        t, u, v, d, s = ((t1, u1, v1, d1, s1), (t2, u2, v2, d2, s2))[k - 1]
        real = mix[k][0].reshape(width, width)
        imag = mix[k][1].reshape(width, width)
        result = jnp.dot(t[...], real, preferred_element_type=F32)
        result = result + jnp.dot(u[...], imag, preferred_element_type=F32)
        v[...] = result.T.astype(BF16)
        result = jnp.dot(real, d[...], preferred_element_type=F32)
        d[...] = (result + jnp.dot(imag, s[...], preferred_element_type=F32)).astype(BF16)

    for copy in far_rows:
        copy.wait_send()
    convolve(0)
    convolve(1)
    convolve(2)

    def rotate_back(target, f0, f1, f2):
        def body(i):
            for degree in range(LMAX + 1):
                extent, kept = 2 * degree + 1, min(degree, MMAX)
                rows = []
                for order in range(-kept, kept + 1):
                    source = (f0, f1, f2)[abs(order)]
                    rs = pl.ds(pl.multiple_of((degree - abs(order)) * 128 + i * 16, 16), 16)
                    lanes = slice(EDGES, 2 * EDGES) if order < 0 else slice(0, EDGES)
                    rows.append(source[rs, lanes].astype(F32).reshape(2, 8, EDGES))
                for n in range(extent):
                    total = None
                    for j, row in enumerate(rows):
                        term = blocks[degree][j, n][None] * row
                        total = term if total is None else total + term
                    first = (degree * degree + n) * 128
                    target[pl.ds(pl.multiple_of(first + i * 16, 16), 16)] = total.reshape(
                        16, EDGES
                    ).astype(BF16)

        steps(8, body)

    rotate_back(rows_b, d0, d1, d2)

    def scatter_back(i):
        total = contract(hot_source, rows_b[wide(i)], 1, 1)
        table_own[:, wide(i)] = total[0:ATOMS]
        table_ghost[:, wide(i)] = total[ATOMS : ATOMS + 2 * GHOSTS]

    steps(7, scatter_back)
    for side in range(2):
        mine = table_ghost[side * GHOSTS : (side + 1) * GHOSTS]
        back_send[side] = jnp.concatenate([mine[:, :PACK], mine[:, WIDTH - PACK :]], 0).astype(BF16)
    back_copies = [
        send(back_send.at[0], back_recv.at[0], to_prev),
        send(back_send.at[1], back_recv.at[1], to_next),
    ]

    rotate_back(rows_f, v0, v1, v2)

    def scatter(i):
        total = contract(hot_target, rows_f[wide(i)], 1, 1)
        updated[:, wide(i)] = (
            features[:, wide(i)].astype(F32) + MESSAGE_SCALE * total
        ).astype(BF16)

    steps(7, scatter)

    for k in range(3):
        finish_grads(k)

    for copy in back_copies:
        copy.wait_recv()
    came = [back_recv[side].astype(F32) for side in range(2)]
    spots = (
        lax.broadcasted_iota(jnp.int32, (ATOMS, 2 * GHOSTS), 0) == ghost_row[...]
    ).astype(BF16)
    for low, high, first, cut in ((0, PACK, 0, 0), (PACK, WIDTH, GHOSTS, 2 * PACK - WIDTH)):
        both = [a[first : first + GHOSTS, cut : cut + high - low] for a in came]
        both = jnp.concatenate(both, 0).astype(BF16)
        total = grad_out[:, low:high].astype(F32) + table_own[:, low:high]
        total = total + jnp.dot(spots, both, preferred_element_type=F32)
        grad_features[:, low:high] = total.astype(BF16)

    for copy in copies:
        if not any(copy is other for other in far_rows):
            copy.wait_send()


def on_device(
    features, grad_out, wigner, sources, targets, ghost_index, edge_count, mixture,
    w_zero, w_one, w_two,
):
    def buffers(*lead):
        shapes = []
        for k in range(3):
            mats = () if k == 0 else (2,)
            shapes.append(pltpu.VMEM(mats + lead + (ROWS[k], COLS[k]), BF16))
        return shapes

    raw = [
        pltpu.VMEM((3, 2) + (() if k == 0 else (2,)) + (ROWS[k], COLS[k]), BF16) for k in range(3)
    ]
    frame = [
        pltpu.VMEM((896, EDGES), BF16),
        pltpu.VMEM((768, 2 * EDGES), BF16),
        pltpu.VMEM((640, 2 * EDGES), BF16),
    ]
    turned = [
        pltpu.VMEM((EDGES, 896), BF16),
        pltpu.VMEM((2 * EDGES, 768), BF16),
        pltpu.VMEM((2 * EDGES, 640), BF16),
    ]
    exchange = [pltpu.VMEM((2, 2 * GHOSTS, PACK), BF16)] * 4
    scratch = (
        raw
        + buffers(4)
        + buffers() * 3
        + buffers(2, 4)
        + buffers(4)
        + buffers() * 3
        + [
            pltpu.VMEM((ATOMS, WIDTH), BF16),
            pltpu.VMEM((WIG_READ, EDGES), BF16),
            pltpu.VMEM((ATOMS, EDGES), BF16),
            pltpu.VMEM((ATOMS, EDGES), BF16),
            pltpu.VMEM((448, EDGES), BF16),
            pltpu.VMEM((384, 2 * EDGES), BF16),
            pltpu.VMEM((320, 2 * EDGES), BF16),
        ]
        + exchange
        + [pltpu.VMEM((WIG_READ, EDGES), F32)]
        + [
            pltpu.VMEM((2 * min(degree, MMAX) + 1, 2 * degree + 1, 8, EDGES), F32)
            for degree in range(LMAX + 1)
        ]
        * 2
        + [pltpu.VMEM((ATOMS + 2 * GHOSTS, WIDTH), BF16)]
        + [pltpu.VMEM((WIDTH, EDGES), BF16)] * 3
        + frame * 3
        + frame[1:] * 2
        + turned
        + turned[1:]
        + [pltpu.VMEM((ATOMS, WIDTH), F32), pltpu.VMEM((2 * GHOSTS, WIDTH), F32)]
        + [pltpu.SemaphoreType.DMA((COPIES,))] * 2
    )
    vmem = pl.BlockSpec(memory_space=pltpu.VMEM)
    smem = pl.BlockSpec(memory_space=pltpu.SMEM)
    return pl.pallas_call(
        kernel,
        out_shape=(
            jax.ShapeDtypeStruct((ATOMS, WIDTH), BF16),
            jax.ShapeDtypeStruct((ATOMS, WIDTH), BF16),
            jax.ShapeDtypeStruct((1, 112, 896), BF16),
            jax.ShapeDtypeStruct((1, 2, 96, 768), BF16),
            jax.ShapeDtypeStruct((1, 2, 80, 640), BF16),
        ),
        in_specs=[smem, smem] + [vmem] * 10,
        out_specs=(vmem,) * 5,
        scratch_shapes=scratch,
        compiler_params=pltpu.CompilerParams(
            collective_id=0, has_side_effects=True, vmem_limit_bytes=58 * 1024 * 1024
        ),
        name="message_layer",
    )(
        mixture,
        edge_count,
        features,
        grad_out,
        wigner,
        sources.reshape(1, -1),
        targets.reshape(1, -1),
        ghost_index.reshape(-1, 1),
        ghost_index.reshape(1, -1),
        w_zero,
        w_one,
        w_two,
    )


def solution(mesh):
    both = ("dp", "space")
    return jax.shard_map(
        on_device,
        mesh=mesh,
        in_specs=(
            P(both, None),
            P(both, None),
            P(None, both),
            P(both),
            P(both),
            P(both, None, None),
            P("dp", "space"),
            P(),
            P("dp", "space", None),
            P("dp", None, "space", None),
            P("dp", None, "space", None),
        ),
        out_specs=(
            P(both, None),
            P(both, None),
            P("dp", "space", None),
            P("dp", None, "space", None),
            P("dp", None, "space", None),
        ),
        check_vma=False,
    )
```

```python
import functools

import jax
import jax.numpy as jnp
from jax import lax
from jax.experimental import pallas as pl
from jax.experimental.pallas import tpu as pltpu
from jax.sharding import PartitionSpec as P

BF16 = jnp.bfloat16
F32 = jnp.float32
MESH = pl.DeviceIdType.MESH

LMAX = 6
MMAX = 2
EDGES = 128
ATOMS = 32
GHOSTS = 8
WIDTH = 6272
PACK = 3200
WIG_READ = 416
MESSAGE_SCALE = 0.25
WEIGHT_SCALE = 1024.0 ** -0.5

ROWS = (112, 96, 80)
COLS = (896, 768, 640)
MATS = (1, 2, 2)
PARTS = (
    ((0, 0, 48, True), (0, 48, 64, False)),
    ((0, 0, 96, True), (1, 0, 96, False)),
    ((0, 0, 80, True), (1, 0, 80, False)),
)
COPIES = 128


def contract(left, right, left_dim, right_dim):
    return lax.dot_general(
        left, right, (((left_dim,), (right_dim,)), ((), ())), preferred_element_type=F32
    )


def whole(ref, chunk, lead):
    return ref.at[lead] if chunk == 0 else ref.at[(slice(None),) + lead]


def steps(count, body):
    def step(i, carry):
        body(i)
        return carry

    lax.fori_loop(0, count, step, 0)


def tiles16(i):
    return pl.ds(pl.multiple_of(i * 16, 16), 16)


def kernel(
    mixture, count, features, grad_out, wigner, sources, targets, ghost_col, ghost_row, w0, w1, w2,
    updated, grad_features, out0, out1, out2,
    raw0, raw1, raw2, par0, par1, par2, za0, za1, za2, mix0, mix1, mix2,
    keep0, keep1, keep2, cs0, cs1, cs2, cx0, cx1, cx2,
    far_grad, far_wigner, hot_send, far_hot, far_v0, far_v1, far_v2,
    ghost_send, ghost_recv, back_send, back_recv,
    wig32, blk0, blk1, blk2, blk3, blk4, blk5, blk6, fbk0, fbk1, fbk2, fbk3, fbk4, fbk5, fbk6,
    table, rows_f, rows_b, rows_p, v0, v1, v2, d0, d1, d2, p0, p1, p2, s1, s2, q1, q2, t0, t1, t2, u1, u2,
    table_own, table_ghost, send_sem, recv_sem,
):
    w = (w0, w1, w2)
    raw = (raw0, raw1, raw2)
    par = (par0, par1, par2)
    za = (za0, za1, za2)
    mix = (mix0, mix1, mix2)
    keep, cs, cx = (keep0, keep1, keep2), (cs0, cs1, cs2), (cx0, cx1, cx2)
    far_v = (far_v0, far_v1, far_v2)
    out = (out0, out1, out2)
    blocks = (blk0, blk1, blk2, blk3, blk4, blk5, blk6)
    far_blocks = (fbk0, fbk1, fbk2, fbk3, fbk4, fbk5, fbk6)

    dp, sp = lax.axis_index("dp"), lax.axis_index("space")
    core, z, xl = dp % 2, (dp // 2) % 4, dp // 8
    y, xh = sp % 4, sp // 4
    dp_core = dp + 1 - 2 * core
    dp_x = (1 - xl) * 8 + z * 2 + core
    dp_xc = (1 - xl) * 8 + z * 2 + 1 - core
    sp_x = (1 - xh) * 4 + y

    def at_z(step):
        return xl * 8 + ((z + step) % 4) * 2 + core

    def at_y(step):
        return xh * 4 + (y + step) % 4

    to_core, to_x = (dp_core, sp), (dp_x, sp)
    along_z = tuple((at_z(step), sp) for step in (1, 2, 3))
    along_y = tuple((dp, at_y(step)) for step in (1, 2, 3))
    to_far = (dp, sp_x)
    to_next, to_prev = (dp, (sp + 1) % 8), (dp, (sp + 7) % 8)
    partners = (to_core, to_x, to_far, to_next, to_prev) + along_z + along_y

    barrier = pltpu.get_barrier_semaphore()
    for partner in partners:
        pl.semaphore_signal(barrier, inc=1, device_id=partner, device_id_type=MESH)

    copies = []

    def send(source, target, device):
        index = len(copies)
        copy = pltpu.make_async_remote_copy(
            src_ref=source,
            dst_ref=target,
            send_sem=send_sem.at[index],
            recv_sem=recv_sem.at[index],
            device_id=device,
            device_id_type=MESH,
        )
        copy.start()
        copies.append(copy)
        return copy

    atom_lane = lax.broadcasted_iota(jnp.int32, (2 * GHOSTS, ATOMS), 1)
    pick = (atom_lane == ghost_col[...]).astype(BF16)
    ghosts = jnp.dot(pick, features[...], preferred_element_type=F32)
    for side in range(2):
        mine = ghosts[side * GHOSTS : (side + 1) * GHOSTS]
        ghost_send[side] = jnp.concatenate([mine[:, :PACK], mine[:, WIDTH - PACK :]], 0).astype(BF16)

    live = lax.broadcasted_iota(jnp.int32, (ATOMS, EDGES), 1) < count[0, 0]
    hot_target = (
        (lax.broadcasted_iota(jnp.int32, (ATOMS, EDGES), 0) == targets[...]) & live
    ).astype(F32)
    hot_quarter = (MESSAGE_SCALE * hot_target).astype(BF16)
    hot_target = hot_target.astype(BF16)
    hot_source = (
        lax.broadcasted_iota(jnp.int32, (ATOMS + 2 * GHOSTS, EDGES), 0) == sources[...]
    ).astype(BF16)

    hot_send[...] = hot_quarter

    pl.semaphore_wait(barrier, len(partners))

    ghost_copies = [
        send(ghost_send.at[0], ghost_recv.at[0], to_next),
        send(ghost_send.at[1], ghost_recv.at[1], to_prev),
    ]
    raw_x, raw_core, raw_xc = {}, {}, {}
    grad_copies = []
    for k in range(3):
        raw_x[k] = send(w[k], raw[k].at[1], to_x)
        raw_core[k] = send(w[k], raw[k].at[0], to_core)
        if k == 0:
            for at in (0, 2):
                grad_copies += [
                    send(grad_out, far_grad.at[at], along_y[at]),
                    send(wigner.at[0:WIG_READ], far_wigner.at[at], along_y[at]),
                    send(hot_send, far_hot.at[at], along_y[at]),
                ]

    def forward_raw(k):
        raw_x[k].wait_recv()
        raw_xc[k] = send(raw[k].at[1], raw[k].at[2], to_core)

    z_sums = {}

    def partials(k):
        raw_core[k].wait_recv()
        raw_xc[k].wait_recv()
        across = COLS[k] // 128
        scale = [
            [
                mixture[(xl * 4 + (z + step) % 4) * 2 + core, 2 * owner + i]
                for owner in (dp, dp_core, dp_x, dp_xc)
                for i in range(2)
            ]
            for step in range(4)
        ]
        for mat in range(MATS[k]):
            lead = () if k == 0 else (mat,)

            def body(t, mat=mat, lead=lead):
                rs = tiles16(t // across)
                c = pl.ds(pl.multiple_of((t % across) * 128, 128), 128)
                terms = [w[k][(i,) + lead + (rs, c)].astype(F32) for i in range(2)]
                for slot in range(3):
                    terms += [raw[k][(slot, i) + lead + (rs, c)].astype(F32) for i in range(2)]
                for step in range(4):
                    total = scale[step][0] * terms[0]
                    for factor, term in zip(scale[step][1:], terms[1:]):
                        total = total + factor * term
                    par[k][lead + (step, rs, c)] = total.astype(BF16)

            steps(ROWS[k] // 16 * across, body)
        z_sums[k] = [
            send(whole(par[k], k, (at + 1,)), whole(za[k], k, (at,)), along_z[at]) for at in (0, 2, 1)
        ]

    def add_up(target, terms, rows, kind=BF16):
        def body(i):
            rs = tiles16(i)
            total = terms[0][rs].astype(F32)
            for term in terms[1:]:
                total = total + term[rs].astype(F32)
            target[rs] = total.astype(kind)

        steps(rows // 16, body)

    def matrix(ref, k, mat, lead):
        return ref.at[lead] if k == 0 else ref.at[(mat,) + lead]

    b_far, b_along = {}, {}

    def spread(k, own):
        place = xh if own else 1 - xh
        here = whole(mix[k], k, (place, y))
        b_along[k, own] = [send(here, here, along_y[at]) for at in (0, 2)]

    def finish_mix(k):
        for copy in z_sums[k]:
            copy.wait_recv()
        for mat in range(MATS[k]):
            terms = [matrix(par[k], k, mat, (0,))]
            terms += [matrix(za[k], k, mat, (at,)) for at in range(3)]
            add_up(matrix(mix[k], k, mat, (xh, y)), terms, ROWS[k])
        here = whole(mix[k], k, (xh, y))
        b_far[k] = send(here, here, to_far)
        spread(k, True)

    def spread_far(k):
        b_far[k].wait_recv()
        spread(k, False)

    b_relay = {}

    def relay_mix(k, own):
        place = xh if own else 1 - xh
        for copy in b_along[k, own]:
            copy.wait_recv()
        b_relay[k, own] = []
        for mat, first, rows, up in PARTS[k]:
            source = matrix(mix[k], k, mat, (place, (y + (3 if up else 1)) % 4))
            source = source.at[pl.ds(first, rows)]
            b_relay[k, own].append(send(source, source, along_y[0 if up else 2]))

    v_copies = []
    c_far = {}

    def send_rows():
        for k, source in enumerate((v0, v1, v2)):
            rows = ROWS[k]
            for at in (0, 2, 1):
                for side in range(2):
                    first = (side * 4 + (y + at + 1) % 4) * rows
                    part = source.at[pl.ds(pl.multiple_of(first, 16), rows)]
                    v_copies.append(send(part, far_v[k].at[at, side], along_y[at]))

    def weight_grads(k):
        rows = ROWS[k]
        v, d, p = ((v0, d0, p0), (v1, d1, p1), (v2, d2, p2))[k]
        swapped = (None, (s1, q1), (s2, q2))[k]
        for mat in range(MATS[k]):
            near, far = (d, p) if mat == 0 else swapped

            def sums(side):
                own = v[pl.ds(pl.multiple_of((side * 4 + y) * rows, 16), rows)]
                total = contract(own, near[...], 1, 1)
                for at in range(3):
                    total = total + contract(far_v[k][at, side], far[at], 1, 1)
                return WEIGHT_SCALE * total

            lead = () if k == 0 else (mat,)
            cs[k][lead + (slice(None),)] = sums(1 - xh).astype(BF16)
            keep[k][lead + (slice(None),)] = sums(xh)
        c_far[k] = send(cs[k], cx[k], to_far)

    def finish_grads(k):
        c_far[k].wait_recv()
        for mat in range(MATS[k]):
            target = out[k].at[(0,) if k == 0 else (0, mat)]
            add_up(target, [matrix(keep[k], k, mat, ()), matrix(cx[k], k, mat, ())], ROWS[k])

    def expand(matrix, target):
        wig32[...] = matrix[0:WIG_READ].astype(F32)
        for degree in range(LMAX + 1):
            extent, kept = 2 * degree + 1, min(degree, MMAX)
            start = degree * (2 * degree - 1) * (2 * degree + 1) // 3 + (degree - kept) * extent
            for j in range(2 * kept + 1):
                rows = wig32[start + j * extent : start + (j + 1) * extent]
                target[degree][j] = jnp.broadcast_to(rows[:, None, :], (extent, 8, EDGES))

    expand(wigner, blocks)

    def wide(i):
        return pl.ds(pl.multiple_of(i * 896, 128), 896)

    def back_gather(i):
        rows_b[wide(i)] = contract(grad_out[:, wide(i)], hot_quarter, 0, 0).astype(BF16)

    steps(7, back_gather)

    for copy in ghost_copies:
        copy.wait_recv()
    table[0:ATOMS] = features[...]
    came = [ghost_recv[side].astype(F32) for side in range(2)]
    for low, high, first, cut in ((0, PACK, 0, 0), (PACK, WIDTH, GHOSTS, 2 * PACK - WIDTH)):
        both = [a[first : first + GHOSTS, cut : cut + high - low] for a in came]
        table[ATOMS : ATOMS + 2 * GHOSTS, low:high] = jnp.concatenate(both, 0).astype(BF16)

    def gather(i):
        rows_f[wide(i)] = contract(table[:, wide(i)], hot_source, 0, 0).astype(BF16)

    steps(7, gather)

    def rotate_into(i, frames, matrices):
        for source, f0, f1, f2 in frames:
            for degree in range(LMAX + 1):
                kept = min(degree, MMAX)
                total = None
                for n in range(2 * degree + 1):
                    first = (degree * degree + n) * 128
                    row = source[pl.ds(pl.multiple_of(first + i * 16, 16), 16)].astype(F32)
                    factor = matrices[degree][:, n]
                    term = factor[:, None] * row.reshape(1, 2, 8, EDGES)
                    total = term if total is None else total + term
                result = total.reshape(2 * kept + 1, 16, EDGES).astype(BF16)
                f0[pl.ds(pl.multiple_of(degree * 128 + i * 16, 16), 16)] = result[kept]
                for order, target in ((1, f1), (2, f2)):
                    if kept >= order:
                        rs = pl.ds(pl.multiple_of((degree - order) * 128 + i * 16, 16), 16)
                        target[rs, 0:EDGES] = result[kept + order]
                        target[rs, EDGES : 2 * EDGES] = result[kept - order]

    steps(8, lambda i: rotate_into(i, ((rows_f, v0, v1, v2), (rows_b, d0, d1, d2)), blocks))
    send_rows()
    def swap(source, target):
        target[:, 0:EDGES] = source[:, EDGES : 2 * EDGES]
        target[:, EDGES : 2 * EDGES] = -source[:, 0:EDGES]

    def turn_frames():
        swap(d1, s1)
        swap(d2, s2)
        t0[...] = v0[...].T
        for source, target, swapped in ((v1, t1, u1), (v2, t2, u2)):
            target[...] = source[...].T
            swapped[0:EDGES] = -target[EDGES : 2 * EDGES]
            swapped[EDGES : 2 * EDGES] = target[0:EDGES]

    def far_frame(at):
        if at == 1:
            for copy in arrivals[1]:
                copy.wait_recv()
        expand(far_wigner.at[at], far_blocks)
        hot = far_hot[at]

        def far_gather(i):
            rows_p[wide(i)] = contract(far_grad[at, :, wide(i)], hot, 0, 0).astype(BF16)

        steps(7, far_gather)
        frame = (rows_p, p0.at[at], p1.at[at], p2.at[at])
        steps(8, lambda i: rotate_into(i, (frame,), far_blocks))
        swap(p1.at[at], q1.at[at])
        swap(p2.at[at], q2.at[at])

    arrivals = {0: grad_copies[0:3], 2: grad_copies[3:6], 1: []}

    def relay_targets():
        for copy in grad_copies:
            copy.wait_recv()
        for ref, rows in ((far_grad, ATOMS // 2), (far_wigner, WIG_READ // 2), (far_hot, ATOMS // 2)):
            for at, first in ((0, 0), (2, rows)):
                source, target = (ref.at[i, pl.ds(first, rows)] for i in (at, 1))
                arrivals[1].append(send(source, target, along_y[at]))

    forward_raw(0)
    partials(0)
    relay_targets()
    far_frame(0)
    finish_mix(0)
    turn_frames()
    forward_raw(1)
    partials(1)
    spread_far(0)
    relay_mix(0, True)
    far_frame(2)
    relay_mix(0, False)
    forward_raw(2)
    partials(2)
    far_frame(1)
    finish_mix(1)
    for copy in v_copies:
        copy.wait_recv()
    weight_grads(0)
    spread_far(1)
    relay_mix(1, True)
    finish_mix(2)
    weight_grads(1)
    relay_mix(1, False)
    spread_far(2)
    relay_mix(2, True)
    weight_grads(2)
    relay_mix(2, False)

    def convolve(k):
        for copy in b_relay[k, True] + b_relay[k, False]:
            copy.wait_recv()
        width = COLS[k]
        if k == 0:
            weight = mix0[...].reshape(width, width)
            v0[...] = jnp.dot(t0[...], weight, preferred_element_type=F32).T.astype(BF16)
            d0[...] = jnp.dot(weight, d0[...], preferred_element_type=F32).astype(BF16)
            return
        t, u, v, d, s = ((t1, u1, v1, d1, s1), (t2, u2, v2, d2, s2))[k - 1]
        real = mix[k][0].reshape(width, width)
        imag = mix[k][1].reshape(width, width)
        result = jnp.dot(t[...], real, preferred_element_type=F32)
        result = result + jnp.dot(u[...], imag, preferred_element_type=F32)
        v[...] = result.T.astype(BF16)
        result = jnp.dot(real, d[...], preferred_element_type=F32)
        d[...] = (result + jnp.dot(imag, s[...], preferred_element_type=F32)).astype(BF16)

    for copy in v_copies:
        copy.wait_send()
    convolve(0)
    convolve(1)
    convolve(2)

    def rotate_back(target, f0, f1, f2):
        def body(i):
            for degree in range(LMAX + 1):
                extent, kept = 2 * degree + 1, min(degree, MMAX)
                rows = []
                for order in range(-kept, kept + 1):
                    source = (f0, f1, f2)[abs(order)]
                    rs = pl.ds(pl.multiple_of((degree - abs(order)) * 128 + i * 16, 16), 16)
                    lanes = slice(EDGES, 2 * EDGES) if order < 0 else slice(0, EDGES)
                    rows.append(source[rs, lanes].astype(F32).reshape(2, 8, EDGES))
                for n in range(extent):
                    total = None
                    for j, row in enumerate(rows):
                        term = blocks[degree][j, n][None] * row
                        total = term if total is None else total + term
                    first = (degree * degree + n) * 128
                    target[pl.ds(pl.multiple_of(first + i * 16, 16), 16)] = total.reshape(
                        16, EDGES
                    ).astype(BF16)

        steps(8, body)

    rotate_back(rows_b, d0, d1, d2)

    def scatter_back(i):
        total = contract(hot_source, rows_b[wide(i)], 1, 1)
        table_own[:, wide(i)] = total[0:ATOMS]
        table_ghost[:, wide(i)] = total[ATOMS : ATOMS + 2 * GHOSTS]

    steps(7, scatter_back)
    for side in range(2):
        mine = table_ghost[side * GHOSTS : (side + 1) * GHOSTS]
        back_send[side] = jnp.concatenate([mine[:, :PACK], mine[:, WIDTH - PACK :]], 0).astype(BF16)
    back_copies = [
        send(back_send.at[0], back_recv.at[0], to_prev),
        send(back_send.at[1], back_recv.at[1], to_next),
    ]

    rotate_back(rows_f, v0, v1, v2)

    def scatter(i):
        total = contract(hot_target, rows_f[wide(i)], 1, 1)
        updated[:, wide(i)] = (
            features[:, wide(i)].astype(F32) + MESSAGE_SCALE * total
        ).astype(BF16)

    steps(7, scatter)

    for k in range(3):
        finish_grads(k)

    for copy in back_copies:
        copy.wait_recv()
    came = [back_recv[side].astype(F32) for side in range(2)]
    spots = (
        lax.broadcasted_iota(jnp.int32, (ATOMS, 2 * GHOSTS), 0) == ghost_row[...]
    ).astype(BF16)
    for low, high, first, cut in ((0, PACK, 0, 0), (PACK, WIDTH, GHOSTS, 2 * PACK - WIDTH)):
        both = [a[first : first + GHOSTS, cut : cut + high - low] for a in came]
        both = jnp.concatenate(both, 0).astype(BF16)
        total = grad_out[:, low:high].astype(F32) + table_own[:, low:high]
        total = total + jnp.dot(spots, both, preferred_element_type=F32)
        grad_features[:, low:high] = total.astype(BF16)

    for copy in copies:
        if not any(copy is other for other in v_copies):
            copy.wait_send()


def on_device(
    features, grad_out, wigner, sources, targets, ghost_index, edge_count, mixture,
    w_zero, w_one, w_two,
):
    def buffers(*lead, kind=BF16):
        shapes = []
        for k in range(3):
            mats = () if k == 0 else (2,)
            shapes.append(pltpu.VMEM(mats + lead + (ROWS[k], COLS[k]), kind))
        return shapes

    raw = [
        pltpu.VMEM((3, 2) + (() if k == 0 else (2,)) + (ROWS[k], COLS[k]), BF16) for k in range(3)
    ]
    frame = [
        pltpu.VMEM((896, EDGES), BF16),
        pltpu.VMEM((768, 2 * EDGES), BF16),
        pltpu.VMEM((640, 2 * EDGES), BF16),
    ]
    far_frames = [
        pltpu.VMEM((3, 896, EDGES), BF16),
        pltpu.VMEM((3, 768, 2 * EDGES), BF16),
        pltpu.VMEM((3, 640, 2 * EDGES), BF16),
    ]
    turned = [
        pltpu.VMEM((EDGES, 896), BF16),
        pltpu.VMEM((2 * EDGES, 768), BF16),
        pltpu.VMEM((2 * EDGES, 640), BF16),
    ]
    exchange = [pltpu.VMEM((2, 2 * GHOSTS, PACK), BF16)] * 4
    scratch = (
        raw
        + buffers(4)
        + buffers(3)
        + buffers(2, 4)
        + buffers(kind=F32)
        + buffers() * 2
        + [
            pltpu.VMEM((3, ATOMS, WIDTH), BF16),
            pltpu.VMEM((3, WIG_READ, EDGES), BF16),
            pltpu.VMEM((ATOMS, EDGES), BF16),
            pltpu.VMEM((3, ATOMS, EDGES), BF16),
            pltpu.VMEM((3, 2, 112, EDGES), BF16),
            pltpu.VMEM((3, 2, 96, 2 * EDGES), BF16),
            pltpu.VMEM((3, 2, 80, 2 * EDGES), BF16),
        ]
        + exchange
        + [pltpu.VMEM((WIG_READ, EDGES), F32)]
        + [
            pltpu.VMEM((2 * min(degree, MMAX) + 1, 2 * degree + 1, 8, EDGES), F32)
            for degree in range(LMAX + 1)
        ]
        * 2
        + [pltpu.VMEM((ATOMS + 2 * GHOSTS, WIDTH), BF16)]
        + [pltpu.VMEM((WIDTH, EDGES), BF16)] * 3
        + frame * 2
        + far_frames
        + frame[1:]
        + far_frames[1:]
        + turned
        + turned[1:]
        + [pltpu.VMEM((ATOMS, WIDTH), F32), pltpu.VMEM((2 * GHOSTS, WIDTH), F32)]
        + [pltpu.SemaphoreType.DMA((COPIES,))] * 2
    )
    vmem = pl.BlockSpec(memory_space=pltpu.VMEM)
    smem = pl.BlockSpec(memory_space=pltpu.SMEM)
    return pl.pallas_call(
        kernel,
        out_shape=(
            jax.ShapeDtypeStruct((ATOMS, WIDTH), BF16),
            jax.ShapeDtypeStruct((ATOMS, WIDTH), BF16),
            jax.ShapeDtypeStruct((1, 112, 896), BF16),
            jax.ShapeDtypeStruct((1, 2, 96, 768), BF16),
            jax.ShapeDtypeStruct((1, 2, 80, 640), BF16),
        ),
        in_specs=[smem, smem] + [vmem] * 10,
        out_specs=(vmem,) * 5,
        scratch_shapes=scratch,
        compiler_params=pltpu.CompilerParams(
            collective_id=0, has_side_effects=True, vmem_limit_bytes=58 * 1024 * 1024
        ),
        name="message_layer",
    )(
        mixture,
        edge_count,
        features,
        grad_out,
        wigner,
        sources.reshape(1, -1),
        targets.reshape(1, -1),
        ghost_index.reshape(-1, 1),
        ghost_index.reshape(1, -1),
        w_zero,
        w_one,
        w_two,
    )


def solution(mesh):
    both = ("dp", "space")
    return jax.shard_map(
        on_device,
        mesh=mesh,
        in_specs=(
            P(both, None),
            P(both, None),
            P(None, both),
            P(both),
            P(both),
            P(both, None, None),
            P("dp", "space"),
            P(),
            P("dp", "space", None),
            P("dp", None, "space", None),
            P("dp", None, "space", None),
        ),
        out_specs=(
            P(both, None),
            P(both, None),
            P("dp", "space", None),
            P("dp", None, "space", None),
            P("dp", None, "space", None),
        ),
        check_vma=False,
    )
```

```python
import functools

import jax
import jax.numpy as jnp
from jax import lax
from jax.experimental import pallas as pl
from jax.experimental.pallas import tpu as pltpu
from jax.sharding import PartitionSpec as P

BF16 = jnp.bfloat16
F32 = jnp.float32
MESH = pl.DeviceIdType.MESH

LMAX = 6
MMAX = 2
EDGES = 128
ATOMS = 32
GHOSTS = 8
WIDTH = 6272
PACK = 3200
WIG_READ = 416
MESSAGE_SCALE = 0.25
WEIGHT_SCALE = 1024.0 ** -0.5

ROWS = (112, 96, 80)
COLS = (896, 768, 640)
MATS = (1, 2, 2)
PIECES = (
    (0, 0, 0, 48, 32),
    (0, 0, 48, 64, 32),
    (1, 0, 0, 96, 48),
    (1, 1, 0, 96, 48),
    (2, 0, 0, 80, 32),
    (2, 1, 0, 80, 48),
)
COPIES = 192


def contract(left, right, left_dim, right_dim):
    return lax.dot_general(
        left, right, (((left_dim,), (right_dim,)), ((), ())), preferred_element_type=F32
    )


def view(ref, piece, lead, first=0, rows=None):
    k, mat, start, length, _ = piece
    rs = pl.ds(start + first, length if rows is None else rows)
    return ref.at[lead + (rs,)] if k == 0 else ref.at[(mat,) + lead + (rs,)]


def experts(ref, piece, lead=()):
    k, mat, start, length, _ = piece
    lead = lead + (slice(None),)
    return ref.at[lead + (pl.ds(start, length),)] if k == 0 else ref.at[lead + (mat,)]


def steps(count, body):
    def step(i, carry):
        body(i)
        return carry

    lax.fori_loop(0, count, step, 0)


def tiles16(i):
    return pl.ds(pl.multiple_of(i * 16, 16), 16)


def kernel(
    mixture, count, features, grad_out, wigner, sources, targets, ghost_index, w0, w1, w2,
    updated, grad_features, out0, out1, out2,
    raw0, raw1, raw2, par0, par1, par2, za0, za1, za2, mix0, mix1, mix2,
    keep0, keep1, keep2, cs0, cs1, cs2, cx0, cx1, cx2,
    far_grad, far_wigner, hot_send, far_hot, far_v0, far_v1, far_v2,
    ghost_send, ghost_recv, back_send, back_recv,
    wig32, blk0, blk1, blk2, blk3, blk4, blk5, blk6, fbk0, fbk1, fbk2, fbk3, fbk4, fbk5, fbk6,
    table, rows_f, rows_b, rows_p, v0, v1, v2, d0, d1, d2, p0, p1, p2, s1, s2, q1, q2, t0, t1, t2, u1, u2,
    table_own, table_ghost, send_sem, recv_sem,
):
    w = (w0, w1, w2)
    raw = (raw0, raw1, raw2)
    par = (par0, par1, par2)
    za = (za0, za1, za2)
    mix = (mix0, mix1, mix2)
    keep, cs, cx = (keep0, keep1, keep2), (cs0, cs1, cs2), (cx0, cx1, cx2)
    far_v = (far_v0, far_v1, far_v2)
    out = (out0, out1, out2)
    blocks = (blk0, blk1, blk2, blk3, blk4, blk5, blk6)
    far_blocks = (fbk0, fbk1, fbk2, fbk3, fbk4, fbk5, fbk6)

    dp, sp = lax.axis_index("dp"), lax.axis_index("space")
    core, z, xl = dp % 2, (dp // 2) % 4, dp // 8
    y, xh = sp % 4, sp // 4
    dp_core = dp + 1 - 2 * core
    dp_x = (1 - xl) * 8 + z * 2 + core
    dp_xc = (1 - xl) * 8 + z * 2 + 1 - core
    sp_x = (1 - xh) * 4 + y

    def at_z(step):
        return xl * 8 + ((z + step) % 4) * 2 + core

    def at_y(step):
        return xh * 4 + (y + step) % 4

    to_core, to_x = (dp_core, sp), (dp_x, sp)
    along_z = tuple((at_z(step), sp) for step in (1, 2, 3))
    along_y = tuple((dp, at_y(step)) for step in (1, 2, 3))
    to_far = (dp, sp_x)
    to_next, to_prev = (dp, (sp + 1) % 8), (dp, (sp + 7) % 8)
    partners = (to_core, to_x, to_far, to_next, to_prev) + along_z + along_y

    barrier = pltpu.get_barrier_semaphore()
    for partner in partners:
        pl.semaphore_signal(barrier, inc=1, device_id=partner, device_id_type=MESH)

    copies = []

    def send(source, target, device):
        index = len(copies)
        copy = pltpu.make_async_remote_copy(
            src_ref=source,
            dst_ref=target,
            send_sem=send_sem.at[index],
            recv_sem=recv_sem.at[index],
            device_id=device,
            device_id_type=MESH,
        )
        copy.start()
        copies.append(copy)
        return copy

    atom = lax.broadcasted_iota(jnp.int32, (ATOMS, GHOSTS), 0)
    spots = jnp.concatenate(
        [(atom == ghost_index[0, side : side + 1]).astype(F32) for side in range(2)], 1
    )
    ghosts = jnp.dot(spots.T.astype(BF16), features[...], preferred_element_type=F32)
    spots = spots.astype(BF16)
    for side in range(2):
        mine = ghosts[side * GHOSTS : (side + 1) * GHOSTS]
        ghost_send[side] = jnp.concatenate([mine[:, :PACK], mine[:, WIDTH - PACK :]], 0).astype(BF16)

    live = lax.broadcasted_iota(jnp.int32, (ATOMS, EDGES), 1) < count[0, 0]
    hot_target = (
        (lax.broadcasted_iota(jnp.int32, (ATOMS, EDGES), 0) == targets[...]) & live
    ).astype(F32)
    hot_quarter = (MESSAGE_SCALE * hot_target).astype(BF16)
    hot_target = hot_target.astype(BF16)
    hot_source = (
        lax.broadcasted_iota(jnp.int32, (ATOMS + 2 * GHOSTS, EDGES), 0) == sources[...]
    ).astype(BF16)

    hot_send[...] = hot_quarter

    pl.semaphore_wait(barrier, len(partners))

    ghost_copies = [
        send(ghost_send.at[0], ghost_recv.at[0], to_next),
        send(ghost_send.at[1], ghost_recv.at[1], to_prev),
    ]
    raw_x, raw_core, raw_xc = {}, {}, {}
    grad_copies = []
    for i, piece in enumerate(PIECES):
        k = piece[0]
        raw_x[i] = send(experts(w[k], piece), experts(raw[k], piece, (1,)), to_x)
        raw_core[i] = send(experts(w[k], piece), experts(raw[k], piece, (0,)), to_core)
        if i == 0:
            for at in (0, 2):
                grad_copies += [
                    send(grad_out, far_grad.at[at], along_y[at]),
                    send(wigner.at[0:WIG_READ], far_wigner.at[at], along_y[at]),
                    send(hot_send, far_hot.at[at], along_y[at]),
                ]

    def forward_raw(i):
        piece = PIECES[i]
        raw_x[i].wait_recv()
        here = raw[piece[0]]
        raw_xc[i] = send(experts(here, piece, (1,)), experts(here, piece, (2,)), to_core)

    z_sums = {}

    def partials(i):
        piece = PIECES[i]
        k, mat, start, length, _ = piece
        raw_core[i].wait_recv()
        raw_xc[i].wait_recv()
        across = COLS[k] // 128
        scale = [
            [
                mixture[(xl * 4 + (z + step) % 4) * 2 + core, 2 * owner + i]
                for owner in (dp, dp_core, dp_x, dp_xc)
                for i in range(2)
            ]
            for step in range(4)
        ]
        lead = () if k == 0 else (mat,)

        def body(t):
            rs = pl.ds(pl.multiple_of(start + t // across * 16, 16), 16)
            c = pl.ds(pl.multiple_of((t % across) * 128, 128), 128)
            terms = [w[k][(i,) + lead + (rs, c)].astype(F32) for i in range(2)]
            for slot in range(3):
                terms += [raw[k][(slot, i) + lead + (rs, c)].astype(F32) for i in range(2)]
            for step in range(4):
                total = scale[step][0] * terms[0]
                for factor, term in zip(scale[step][1:], terms[1:]):
                    total = total + factor * term
                par[k][lead + (step, rs, c)] = total.astype(BF16)

        steps(length // 16 * across, body)
        z_sums[i] = [
            send(view(par[k], piece, (at + 1,)), view(za[k], piece, (at,)), along_z[at])
            for at in (0, 2, 1)
        ]

    def add_up(target, terms, rows, kind=BF16):
        def body(i):
            rs = tiles16(i)
            total = terms[0][rs].astype(F32)
            for term in terms[1:]:
                total = total + term[rs].astype(F32)
            target[rs] = total.astype(kind)

        steps(rows // 16, body)

    def matrix(ref, k, mat, lead):
        return ref.at[lead] if k == 0 else ref.at[(mat,) + lead]

    b_far, b_along = {}, {}

    def spread(i, own):
        piece = PIECES[i]
        here = view(mix[piece[0]], piece, (xh if own else 1 - xh, y))
        b_along[i, own] = [send(here, here, along_y[at]) for at in (0, 2)]

    def finish_mix(i):
        piece = PIECES[i]
        k = piece[0]
        for copy in z_sums[i]:
            copy.wait_recv()
        here = view(mix[k], piece, (xh, y))
        terms = [view(par[k], piece, (0,))] + [view(za[k], piece, (at,)) for at in range(3)]
        add_up(here, terms, piece[3])
        b_far[i] = send(here, here, to_far)
        spread(i, True)

    def spread_far(i):
        b_far[i].wait_recv()
        spread(i, False)

    b_relay = {}

    def relay_mix(i, own):
        piece = PIECES[i]
        k, _, _, length, upward = piece
        place = xh if own else 1 - xh
        b_relay[i, own] = []
        for copy in b_along[i, own]:
            copy.wait_recv()
        for at, step, first, rows in ((0, 3, 0, upward), (2, 1, upward, length - upward)):
            here = view(mix[k], piece, (place, (y + step) % 4), first, rows)
            b_relay[i, own].append(send(here, here, along_y[at]))

    v_copies = []
    c_far = {}

    def send_rows():
        for k, source in enumerate((v0, v1, v2)):
            rows = ROWS[k]
            for at in (0, 2, 1):
                for side in range(2):
                    first = (side * 4 + (y + at + 1) % 4) * rows
                    part = source.at[pl.ds(pl.multiple_of(first, 16), rows)]
                    v_copies.append(send(part, far_v[k].at[at, side], along_y[at]))

    def weight_grads(k):
        rows = ROWS[k]
        v, d, p = ((v0, d0, p0), (v1, d1, p1), (v2, d2, p2))[k]
        swapped = (None, (s1, q1), (s2, q2))[k]
        for mat in range(MATS[k]):
            near, far = (d, p) if mat == 0 else swapped

            def sums(side):
                own = v[pl.ds(pl.multiple_of((side * 4 + y) * rows, 16), rows)]
                total = contract(own, near[...], 1, 1)
                for at in range(3):
                    total = total + contract(far_v[k][at, side], far[at], 1, 1)
                return WEIGHT_SCALE * total

            lead = () if k == 0 else (mat,)
            cs[k][lead + (slice(None),)] = sums(1 - xh).astype(BF16)
            keep[k][lead + (slice(None),)] = sums(xh)
        c_far[k] = send(cs[k], cx[k], to_far)

    def finish_grads(k):
        c_far[k].wait_recv()
        for mat in range(MATS[k]):
            target = out[k].at[(0,) if k == 0 else (0, mat)]
            add_up(target, [matrix(keep[k], k, mat, ()), matrix(cx[k], k, mat, ())], ROWS[k])

    def expand(matrix, target):
        wig32[...] = matrix[0:WIG_READ].astype(F32)
        for degree in range(LMAX + 1):
            extent, kept = 2 * degree + 1, min(degree, MMAX)
            start = degree * (2 * degree - 1) * (2 * degree + 1) // 3 + (degree - kept) * extent
            for j in range(2 * kept + 1):
                rows = wig32[start + j * extent : start + (j + 1) * extent]
                target[degree][j] = jnp.broadcast_to(rows[:, None, :], (extent, 8, EDGES))

    expand(wigner, blocks)

    def wide(i):
        return pl.ds(pl.multiple_of(i * 896, 128), 896)

    def back_gather(i):
        rows_b[wide(i)] = contract(grad_out[:, wide(i)], hot_quarter, 0, 0).astype(BF16)

    steps(7, back_gather)

    for copy in ghost_copies:
        copy.wait_recv()
    table[0:ATOMS] = features[...]
    came = [ghost_recv[side].astype(F32) for side in range(2)]
    for low, high, first, cut in ((0, PACK, 0, 0), (PACK, WIDTH, GHOSTS, 2 * PACK - WIDTH)):
        both = [a[first : first + GHOSTS, cut : cut + high - low] for a in came]
        table[ATOMS : ATOMS + 2 * GHOSTS, low:high] = jnp.concatenate(both, 0).astype(BF16)

    def gather(i):
        rows_f[wide(i)] = contract(table[:, wide(i)], hot_source, 0, 0).astype(BF16)

    steps(7, gather)

    def rotate_into(i, frames, matrices):
        for source, f0, f1, f2 in frames:
            for degree in range(LMAX + 1):
                kept = min(degree, MMAX)
                total = None
                for n in range(2 * degree + 1):
                    first = (degree * degree + n) * 128
                    row = source[pl.ds(pl.multiple_of(first + i * 16, 16), 16)].astype(F32)
                    factor = matrices[degree][:, n]
                    term = factor[:, None] * row.reshape(1, 2, 8, EDGES)
                    total = term if total is None else total + term
                result = total.reshape(2 * kept + 1, 16, EDGES).astype(BF16)
                f0[pl.ds(pl.multiple_of(degree * 128 + i * 16, 16), 16)] = result[kept]
                for order, target in ((1, f1), (2, f2)):
                    if kept >= order:
                        rs = pl.ds(pl.multiple_of((degree - order) * 128 + i * 16, 16), 16)
                        target[rs, 0:EDGES] = result[kept + order]
                        target[rs, EDGES : 2 * EDGES] = result[kept - order]

    forward_raw(0)
    partials(0)
    steps(8, lambda i: rotate_into(i, ((rows_f, v0, v1, v2), (rows_b, d0, d1, d2)), blocks))
    send_rows()
    def swap(source, target):
        target[:, 0:EDGES] = source[:, EDGES : 2 * EDGES]
        target[:, EDGES : 2 * EDGES] = -source[:, 0:EDGES]

    def turn_frames():
        swap(d1, s1)
        swap(d2, s2)
        t0[...] = v0[...].T
        for source, target, swapped in ((v1, t1, u1), (v2, t2, u2)):
            target[...] = source[...].T
            swapped[0:EDGES] = -target[EDGES : 2 * EDGES]
            swapped[EDGES : 2 * EDGES] = target[0:EDGES]

    def far_frame(at):
        if at == 1:
            for copy in arrivals[1]:
                copy.wait_recv()
        expand(far_wigner.at[at], far_blocks)
        hot = far_hot[at]

        def far_gather(i):
            rows_p[wide(i)] = contract(far_grad[at, :, wide(i)], hot, 0, 0).astype(BF16)

        steps(7, far_gather)
        frame = (rows_p, p0.at[at], p1.at[at], p2.at[at])
        steps(8, lambda i: rotate_into(i, (frame,), far_blocks))
        swap(p1.at[at], q1.at[at])
        swap(p2.at[at], q2.at[at])

    arrivals = {0: grad_copies[0:3], 2: grad_copies[3:6], 1: []}

    def relay_targets():
        for copy in grad_copies:
            copy.wait_recv()
        for ref, rows in ((far_grad, ATOMS // 2), (far_wigner, WIG_READ // 2), (far_hot, ATOMS // 2)):
            for at, first in ((0, 0), (2, rows)):
                source, target = (ref.at[i, pl.ds(first, rows)] for i in (at, 1))
                arrivals[1].append(send(source, target, along_y[at]))

    forward_raw(1)
    relay_targets()
    partials(1)
    far_frame(0)
    finish_mix(0)
    forward_raw(2)
    partials(2)
    spread_far(0)
    finish_mix(1)
    relay_mix(0, True)
    turn_frames()
    forward_raw(3)
    partials(3)
    relay_mix(0, False)
    spread_far(1)
    finish_mix(2)
    relay_mix(1, True)
    far_frame(2)
    forward_raw(4)
    partials(4)
    relay_mix(1, False)
    spread_far(2)
    finish_mix(3)
    relay_mix(2, True)
    forward_raw(5)
    partials(5)
    far_frame(1)
    relay_mix(2, False)
    spread_far(3)
    finish_mix(4)
    relay_mix(3, True)
    for copy in v_copies:
        copy.wait_recv()
    weight_grads(0)
    finish_mix(5)
    relay_mix(3, False)
    spread_far(4)
    relay_mix(4, True)
    weight_grads(1)
    spread_far(5)
    relay_mix(4, False)
    relay_mix(5, True)
    weight_grads(2)
    relay_mix(5, False)

    def convolve(k):
        for i, piece in enumerate(PIECES):
            if piece[0] == k:
                for copy in b_relay[i, True] + b_relay[i, False]:
                    copy.wait_recv()
        width = COLS[k]
        if k == 0:
            weight = mix0[...].reshape(width, width)
            v0[...] = jnp.dot(t0[...], weight, preferred_element_type=F32).T.astype(BF16)
            d0[...] = jnp.dot(weight, d0[...], preferred_element_type=F32).astype(BF16)
            return
        t, u, v, d, s = ((t1, u1, v1, d1, s1), (t2, u2, v2, d2, s2))[k - 1]
        real = mix[k][0].reshape(width, width)
        imag = mix[k][1].reshape(width, width)
        result = jnp.dot(t[...], real, preferred_element_type=F32)
        result = result + jnp.dot(u[...], imag, preferred_element_type=F32)
        v[...] = result.T.astype(BF16)
        result = jnp.dot(real, d[...], preferred_element_type=F32)
        d[...] = (result + jnp.dot(imag, s[...], preferred_element_type=F32)).astype(BF16)

    for copy in v_copies:
        copy.wait_send()
    convolve(0)
    convolve(1)
    convolve(2)

    def rotate_back(target, f0, f1, f2):
        def body(i):
            for degree in range(LMAX + 1):
                extent, kept = 2 * degree + 1, min(degree, MMAX)
                rows = []
                for order in range(-kept, kept + 1):
                    source = (f0, f1, f2)[abs(order)]
                    rs = pl.ds(pl.multiple_of((degree - abs(order)) * 128 + i * 16, 16), 16)
                    lanes = slice(EDGES, 2 * EDGES) if order < 0 else slice(0, EDGES)
                    rows.append(source[rs, lanes].astype(F32).reshape(2, 8, EDGES))
                for n in range(extent):
                    total = None
                    for j, row in enumerate(rows):
                        term = blocks[degree][j, n][None] * row
                        total = term if total is None else total + term
                    first = (degree * degree + n) * 128
                    target[pl.ds(pl.multiple_of(first + i * 16, 16), 16)] = total.reshape(
                        16, EDGES
                    ).astype(BF16)

        steps(8, body)

    rotate_back(rows_b, d0, d1, d2)

    def scatter_back(i):
        total = contract(hot_source, rows_b[wide(i)], 1, 1)
        table_own[:, wide(i)] = total[0:ATOMS]
        table_ghost[:, wide(i)] = total[ATOMS : ATOMS + 2 * GHOSTS]

    steps(7, scatter_back)
    for side in range(2):
        mine = table_ghost[side * GHOSTS : (side + 1) * GHOSTS]
        back_send[side] = jnp.concatenate([mine[:, :PACK], mine[:, WIDTH - PACK :]], 0).astype(BF16)
    back_copies = [
        send(back_send.at[0], back_recv.at[0], to_prev),
        send(back_send.at[1], back_recv.at[1], to_next),
    ]

    rotate_back(rows_f, v0, v1, v2)

    def scatter(i):
        total = contract(hot_target, rows_f[wide(i)], 1, 1)
        updated[:, wide(i)] = (
            features[:, wide(i)].astype(F32) + MESSAGE_SCALE * total
        ).astype(BF16)

    steps(7, scatter)

    for k in range(3):
        finish_grads(k)

    for copy in back_copies:
        copy.wait_recv()
    came = [back_recv[side].astype(F32) for side in range(2)]
    for low, high, first, cut in ((0, PACK, 0, 0), (PACK, WIDTH, GHOSTS, 2 * PACK - WIDTH)):
        both = [a[first : first + GHOSTS, cut : cut + high - low] for a in came]
        both = jnp.concatenate(both, 0).astype(BF16)
        total = grad_out[:, low:high].astype(F32) + table_own[:, low:high]
        total = total + jnp.dot(spots, both, preferred_element_type=F32)
        grad_features[:, low:high] = total.astype(BF16)

    for copy in copies:
        if not any(copy is other for other in v_copies):
            copy.wait_send()


def copy_out(*refs):
    copies = [pltpu.make_async_copy(refs[i], refs[5 + i], refs[10].at[i]) for i in range(5)]
    for copy in copies:
        copy.start()
    for copy in copies:
        copy.wait()


def on_device(
    features, grad_out, wigner, sources, targets, ghost_index, edge_count, mixture,
    w_zero, w_one, w_two,
):
    def buffers(*lead, kind=BF16):
        shapes = []
        for k in range(3):
            mats = () if k == 0 else (2,)
            shapes.append(pltpu.VMEM(mats + lead + (ROWS[k], COLS[k]), kind))
        return shapes

    raw = [
        pltpu.VMEM((3, 2) + (() if k == 0 else (2,)) + (ROWS[k], COLS[k]), BF16) for k in range(3)
    ]
    frame = [
        pltpu.VMEM((896, EDGES), BF16),
        pltpu.VMEM((768, 2 * EDGES), BF16),
        pltpu.VMEM((640, 2 * EDGES), BF16),
    ]
    far_frames = [
        pltpu.VMEM((3, 896, EDGES), BF16),
        pltpu.VMEM((3, 768, 2 * EDGES), BF16),
        pltpu.VMEM((3, 640, 2 * EDGES), BF16),
    ]
    turned = [
        pltpu.VMEM((EDGES, 896), BF16),
        pltpu.VMEM((2 * EDGES, 768), BF16),
        pltpu.VMEM((2 * EDGES, 640), BF16),
    ]
    exchange = [pltpu.VMEM((2, 2 * GHOSTS, PACK), BF16)] * 4
    scratch = (
        raw
        + buffers(4)
        + buffers(3)
        + buffers(2, 4)
        + buffers(kind=F32)
        + buffers() * 2
        + [
            pltpu.VMEM((3, ATOMS, WIDTH), BF16),
            pltpu.VMEM((3, WIG_READ, EDGES), BF16),
            pltpu.VMEM((ATOMS, EDGES), BF16),
            pltpu.VMEM((3, ATOMS, EDGES), BF16),
            pltpu.VMEM((3, 2, 112, EDGES), BF16),
            pltpu.VMEM((3, 2, 96, 2 * EDGES), BF16),
            pltpu.VMEM((3, 2, 80, 2 * EDGES), BF16),
        ]
        + exchange
        + [pltpu.VMEM((WIG_READ, EDGES), F32)]
        + [
            pltpu.VMEM((2 * min(degree, MMAX) + 1, 2 * degree + 1, 8, EDGES), F32)
            for degree in range(LMAX + 1)
        ]
        * 2
        + [pltpu.VMEM((ATOMS + 2 * GHOSTS, WIDTH), BF16)]
        + [pltpu.VMEM((WIDTH, EDGES), BF16)] * 3
        + frame * 2
        + far_frames
        + frame[1:]
        + far_frames[1:]
        + turned
        + turned[1:]
        + [pltpu.VMEM((ATOMS, WIDTH), F32), pltpu.VMEM((2 * GHOSTS, WIDTH), F32)]
        + [pltpu.SemaphoreType.DMA((COPIES,))] * 2
    )
    vmem = pl.BlockSpec(memory_space=pltpu.VMEM)
    smem = pl.BlockSpec(memory_space=pltpu.SMEM)
    results = pl.pallas_call(
        kernel,
        out_shape=(
            jax.ShapeDtypeStruct((ATOMS, WIDTH), BF16),
            jax.ShapeDtypeStruct((ATOMS, WIDTH), BF16),
            jax.ShapeDtypeStruct((1, 112, 896), BF16),
            jax.ShapeDtypeStruct((1, 2, 96, 768), BF16),
            jax.ShapeDtypeStruct((1, 2, 80, 640), BF16),
        ),
        in_specs=[smem, smem] + [vmem] * 9,
        out_specs=(vmem,) * 5,
        scratch_shapes=scratch,
        compiler_params=pltpu.CompilerParams(
            collective_id=0, has_side_effects=True, vmem_limit_bytes=58 * 1024 * 1024
        ),
        name="message_layer",
    )(
        mixture,
        edge_count,
        features,
        grad_out,
        wigner,
        sources.reshape(1, -1),
        targets.reshape(1, -1),
        ghost_index,
        w_zero,
        w_one,
        w_two,
    )
    anywhere = pl.BlockSpec(memory_space=pl.ANY)
    return pl.pallas_call(
        copy_out,
        out_shape=tuple(jax.ShapeDtypeStruct(a.shape, a.dtype) for a in results),
        in_specs=[vmem] * 5,
        out_specs=(anywhere,) * 5,
        scratch_shapes=[pltpu.SemaphoreType.DMA((5,))],
        name="copy_out",
    )(*results)


def solution(mesh):
    both = ("dp", "space")
    return jax.shard_map(
        on_device,
        mesh=mesh,
        in_specs=(
            P(both, None),
            P(both, None),
            P(None, both),
            P(both),
            P(both),
            P(both, None, None),
            P("dp", "space"),
            P(),
            P("dp", "space", None),
            P("dp", None, "space", None),
            P("dp", None, "space", None),
        ),
        out_specs=(
            P(both, None),
            P(both, None),
            P("dp", "space", None),
            P("dp", None, "space", None),
            P("dp", None, "space", None),
        ),
        check_vma=False,
    )
```

```python
import functools

import jax
import jax.numpy as jnp
from jax import lax
from jax.experimental import pallas as pl
from jax.experimental.pallas import tpu as pltpu
from jax.sharding import PartitionSpec as P

BF16 = jnp.bfloat16
F32 = jnp.float32
MESH = pl.DeviceIdType.MESH

LMAX = 6
MMAX = 2
EDGES = 128
ATOMS = 32
GHOSTS = 8
WIDTH = 6272
PACK = 3200
WIG_READ = 416
MESSAGE_SCALE = 0.25
WEIGHT_SCALE = 1024.0 ** -0.5

ROWS = (112, 96, 80)
COLS = (896, 768, 640)
MATS = (1, 2, 2)
PIECES = (
    (0, 0, 0, 48, 32),
    (0, 0, 48, 64, 32),
    (1, 0, 0, 96, 48),
    (1, 1, 0, 96, 48),
    (2, 0, 0, 80, 32),
    (2, 1, 0, 80, 48),
)
COPIES = 192


def contract(left, right, left_dim, right_dim):
    return lax.dot_general(
        left, right, (((left_dim,), (right_dim,)), ((), ())), preferred_element_type=F32
    )


def view(ref, piece, lead, first=0, rows=None):
    k, mat, start, length, _ = piece
    rs = pl.ds(start + first, length if rows is None else rows)
    return ref.at[lead + (rs,)] if k == 0 else ref.at[(mat,) + lead + (rs,)]


def experts(ref, piece, lead=()):
    k, mat, start, length, _ = piece
    lead = lead + (slice(None),)
    return ref.at[lead + (pl.ds(start, length),)] if k == 0 else ref.at[lead + (mat,)]


def steps(count, body):
    def step(i, carry):
        body(i)
        return carry

    lax.fori_loop(0, count, step, 0)


def tiles16(i):
    return pl.ds(pl.multiple_of(i * 16, 16), 16)


def kernel(
    mixture, count, features, grad_out, wigner, sources, targets, ghost_index, w0, w1, w2,
    updated, grad_features, out0, out1, out2,
    raw0, raw1, raw2, par0, par1, par2, za0, za1, za2, mix0, mix1, mix2,
    keep0, keep1, keep2, cs0, cs1, cs2, cx0, cx1, cx2,
    far_grad, far_wigner, hot_send, far_hot, far_v0, far_v1, far_v2,
    ghost_send, ghost_recv, back_send, back_recv,
    wig32, blk0, blk1, blk2, blk3, blk4, blk5, blk6, fbk0, fbk1, fbk2, fbk3, fbk4, fbk5, fbk6,
    table, rows_f, rows_b, rows_p, v0, v1, v2, d0, d1, d2, p0, p1, p2, s1, s2, q1, q2, t0, t1, t2, u1, u2,
    table_own, table_ghost, send_sem, recv_sem,
):
    w = (w0, w1, w2)
    raw = (raw0, raw1, raw2)
    par = (par0, par1, par2)
    za = (za0, za1, za2)
    mix = (mix0, mix1, mix2)
    keep, cs, cx = (keep0, keep1, keep2), (cs0, cs1, cs2), (cx0, cx1, cx2)
    far_v = (far_v0, far_v1, far_v2)
    out = (out0, out1, out2)
    blocks = (blk0, blk1, blk2, blk3, blk4, blk5, blk6)
    far_blocks = (fbk0, fbk1, fbk2, fbk3, fbk4, fbk5, fbk6)

    dp, sp = lax.axis_index("dp"), lax.axis_index("space")
    core, z, xl = dp % 2, (dp // 2) % 4, dp // 8
    y, xh = sp % 4, sp // 4
    dp_core = dp + 1 - 2 * core
    dp_x = (1 - xl) * 8 + z * 2 + core
    dp_xc = (1 - xl) * 8 + z * 2 + 1 - core
    sp_x = (1 - xh) * 4 + y

    def at_z(step):
        return xl * 8 + ((z + step) % 4) * 2 + core

    def at_y(step):
        return xh * 4 + (y + step) % 4

    to_core, to_x = (dp_core, sp), (dp_x, sp)
    along_z = tuple((at_z(step), sp) for step in (1, 2, 3))
    along_y = tuple((dp, at_y(step)) for step in (1, 2, 3))
    to_far = (dp, sp_x)
    to_next, to_prev = (dp, (sp + 1) % 8), (dp, (sp + 7) % 8)
    partners = (to_core, to_x, to_far, to_next, to_prev) + along_z + along_y

    barrier = pltpu.get_barrier_semaphore()
    for partner in partners:
        pl.semaphore_signal(barrier, inc=1, device_id=partner, device_id_type=MESH)

    copies = []

    def send(source, target, device):
        index = len(copies)
        copy = pltpu.make_async_remote_copy(
            src_ref=source,
            dst_ref=target,
            send_sem=send_sem.at[index],
            recv_sem=recv_sem.at[index],
            device_id=device,
            device_id_type=MESH,
        )
        copy.start()
        copies.append(copy)
        return copy

    atom = lax.broadcasted_iota(jnp.int32, (ATOMS, GHOSTS), 0)
    spots = jnp.concatenate(
        [(atom == ghost_index[0, side : side + 1]).astype(F32) for side in range(2)], 1
    )
    ghosts = jnp.dot(spots.T.astype(BF16), features[...], preferred_element_type=F32)
    spots = spots.astype(BF16)
    for side in range(2):
        mine = ghosts[side * GHOSTS : (side + 1) * GHOSTS]
        ghost_send[side] = jnp.concatenate([mine[:, :PACK], mine[:, WIDTH - PACK :]], 0).astype(BF16)

    live = lax.broadcasted_iota(jnp.int32, (ATOMS, EDGES), 1) < count[0, 0]
    hot_target = (
        (lax.broadcasted_iota(jnp.int32, (ATOMS, EDGES), 0) == targets[...]) & live
    ).astype(F32)
    hot_quarter = (MESSAGE_SCALE * hot_target).astype(BF16)
    hot_target = hot_target.astype(BF16)
    hot_source = (
        lax.broadcasted_iota(jnp.int32, (ATOMS + 2 * GHOSTS, EDGES), 0) == sources[...]
    ).astype(BF16)

    hot_send[...] = hot_quarter

    pl.semaphore_wait(barrier, len(partners))

    ghost_copies = [
        send(ghost_send.at[0], ghost_recv.at[0], to_next),
        send(ghost_send.at[1], ghost_recv.at[1], to_prev),
    ]
    raw_x, raw_core, raw_xc = {}, {}, {}
    grad_copies = []
    for i, piece in enumerate(PIECES):
        k = piece[0]
        raw_x[i] = send(experts(w[k], piece), experts(raw[k], piece, (1,)), to_x)
        raw_core[i] = send(experts(w[k], piece), experts(raw[k], piece, (0,)), to_core)
        if i == 0:
            for at in (0, 2):
                grad_copies += [
                    send(grad_out, far_grad.at[at], along_y[at]),
                    send(wigner.at[0:WIG_READ], far_wigner.at[at], along_y[at]),
                    send(hot_send, far_hot.at[at], along_y[at]),
                ]

    def forward_raw(i):
        piece = PIECES[i]
        raw_x[i].wait_recv()
        here = raw[piece[0]]
        raw_xc[i] = send(experts(here, piece, (1,)), experts(here, piece, (2,)), to_core)

    z_sums = {}

    def partials(i):
        piece = PIECES[i]
        k, mat, start, length, _ = piece
        raw_core[i].wait_recv()
        raw_xc[i].wait_recv()
        across = COLS[k] // 128
        scale = [
            [
                mixture[(xl * 4 + (z + step) % 4) * 2 + core, 2 * owner + i]
                for owner in (dp, dp_core, dp_x, dp_xc)
                for i in range(2)
            ]
            for step in range(4)
        ]
        lead = () if k == 0 else (mat,)

        def body(t):
            rs = pl.ds(pl.multiple_of(start + t * 16, 16), 16)
            for block in range(across):
                c = slice(block * 128, (block + 1) * 128)
                terms = [w[k][(i,) + lead + (rs, c)].astype(F32) for i in range(2)]
                for slot in range(3):
                    terms += [raw[k][(slot, i) + lead + (rs, c)].astype(F32) for i in range(2)]
                for step in range(4):
                    total = scale[step][0] * terms[0]
                    for factor, term in zip(scale[step][1:], terms[1:]):
                        total = total + factor * term
                    par[k][lead + (step, rs, c)] = total.astype(BF16)

        steps(length // 16, body)
        z_sums[i] = [
            send(view(par[k], piece, (at + 1,)), view(za[k], piece, (at,)), along_z[at])
            for at in (0, 2, 1)
        ]

    def add_up(target, terms, rows, kind=BF16):
        def body(i):
            rs = tiles16(i)
            total = terms[0][rs].astype(F32)
            for term in terms[1:]:
                total = total + term[rs].astype(F32)
            target[rs] = total.astype(kind)

        steps(rows // 16, body)

    def matrix(ref, k, mat, lead):
        return ref.at[lead] if k == 0 else ref.at[(mat,) + lead]

    b_far, b_along = {}, {}

    def spread(i, own):
        piece = PIECES[i]
        here = view(mix[piece[0]], piece, (xh if own else 1 - xh, y))
        b_along[i, own] = [send(here, here, along_y[at]) for at in (0, 2)]

    def finish_mix(i):
        piece = PIECES[i]
        k = piece[0]
        for copy in z_sums[i]:
            copy.wait_recv()
        here = view(mix[k], piece, (xh, y))
        terms = [view(par[k], piece, (0,))] + [view(za[k], piece, (at,)) for at in range(3)]
        add_up(here, terms, piece[3])
        b_far[i] = send(here, here, to_far)
        spread(i, True)

    def spread_far(i):
        b_far[i].wait_recv()
        spread(i, False)

    b_relay = {}

    def relay_mix(i, own):
        piece = PIECES[i]
        k, _, _, length, upward = piece
        place = xh if own else 1 - xh
        b_relay[i, own] = []
        for copy in b_along[i, own]:
            copy.wait_recv()
        for at, step, first, rows in ((0, 3, 0, upward), (2, 1, upward, length - upward)):
            here = view(mix[k], piece, (place, (y + step) % 4), first, rows)
            b_relay[i, own].append(send(here, here, along_y[at]))

    v_copies = []
    c_far = {}

    def send_rows():
        for k, source in enumerate((v0, v1, v2)):
            rows = ROWS[k]
            for at in (0, 2, 1):
                for side in range(2):
                    first = (side * 4 + (y + at + 1) % 4) * rows
                    part = source.at[pl.ds(pl.multiple_of(first, 16), rows)]
                    v_copies.append(send(part, far_v[k].at[at, side], along_y[at]))

    def weight_grads(k):
        rows = ROWS[k]
        v, d, p = ((v0, d0, p0), (v1, d1, p1), (v2, d2, p2))[k]
        swapped = (None, (s1, q1), (s2, q2))[k]
        own = [v[pl.ds(pl.multiple_of((side * 4 + y) * rows, 16), rows)] for side in range(2)]
        own = jnp.concatenate(own, 0)
        others = [far_v[k][at].reshape(2 * rows, own.shape[1]) for at in range(3)]
        for mat in range(MATS[k]):
            near, far = (d, p) if mat == 0 else swapped
            total = contract(own, near[...], 1, 1)
            for at in range(3):
                total = total + contract(others[at], far[at], 1, 1)
            total = (WEIGHT_SCALE * total).reshape(2, rows, COLS[k])
            for side in range(2):
                matrix(keep[k], k, mat, (side,))[...] = total[side]
            matrix(cs[k], k, mat, ())[...] = matrix(keep[k], k, mat, (1 - xh,))[...].astype(BF16)
        c_far[k] = send(cs[k], cx[k], to_far)

    def finish_grads(k):
        c_far[k].wait_recv()
        for mat in range(MATS[k]):
            target = out[k].at[(0,) if k == 0 else (0, mat)]
            add_up(target, [matrix(keep[k], k, mat, (xh,)), matrix(cx[k], k, mat, ())], ROWS[k])

    def expand(matrix, target):
        wig32[...] = matrix[0:WIG_READ].astype(F32)
        for degree in range(LMAX + 1):
            extent, kept = 2 * degree + 1, min(degree, MMAX)
            start = degree * (2 * degree - 1) * (2 * degree + 1) // 3 + (degree - kept) * extent
            for j in range(2 * kept + 1):
                rows = wig32[start + j * extent : start + (j + 1) * extent]
                target[degree][j] = jnp.broadcast_to(rows[:, None, :], (extent, 8, EDGES))

    expand(wigner, blocks)

    def wide(i):
        return slice(i * 896, (i + 1) * 896)

    def back_gather(i):
        rows_b[wide(i)] = contract(grad_out[:, wide(i)], hot_quarter, 0, 0).astype(BF16)

    for i in range(7):
        back_gather(i)

    for copy in ghost_copies:
        copy.wait_recv()
    table[0:ATOMS] = features[...]
    came = [ghost_recv[side].astype(F32) for side in range(2)]
    for low, high, first, cut in ((0, PACK, 0, 0), (PACK, WIDTH, GHOSTS, 2 * PACK - WIDTH)):
        both = [a[first : first + GHOSTS, cut : cut + high - low] for a in came]
        table[ATOMS : ATOMS + 2 * GHOSTS, low:high] = jnp.concatenate(both, 0).astype(BF16)

    def gather(i):
        rows_f[wide(i)] = contract(table[:, wide(i)], hot_source, 0, 0).astype(BF16)

    for i in range(7):
        gather(i)

    def rotate_into(i, frames, matrices):
        for source, f0, f1, f2 in frames:
            for degree in range(LMAX + 1):
                kept = min(degree, MMAX)
                total = None
                for n in range(2 * degree + 1):
                    first = (degree * degree + n) * 128
                    row = source[pl.ds(pl.multiple_of(first + i * 16, 16), 16)].astype(F32)
                    factor = matrices[degree][:, n]
                    term = factor[:, None] * row.reshape(1, 2, 8, EDGES)
                    total = term if total is None else total + term
                result = total.reshape(2 * kept + 1, 16, EDGES).astype(BF16)
                f0[pl.ds(pl.multiple_of(degree * 128 + i * 16, 16), 16)] = result[kept]
                for order, target in ((1, f1), (2, f2)):
                    if kept >= order:
                        rs = pl.ds(pl.multiple_of((degree - order) * 128 + i * 16, 16), 16)
                        target[rs, 0:EDGES] = result[kept + order]
                        target[rs, EDGES : 2 * EDGES] = result[kept - order]

    forward_raw(0)
    partials(0)
    steps(8, lambda i: rotate_into(i, ((rows_f, v0, v1, v2), (rows_b, d0, d1, d2)), blocks))
    send_rows()
    def swap(source, target):
        target[:, 0:EDGES] = source[:, EDGES : 2 * EDGES]
        target[:, EDGES : 2 * EDGES] = -source[:, 0:EDGES]

    def turn_frames():
        swap(d1, s1)
        swap(d2, s2)
        t0[...] = v0[...].T
        for source, target, swapped in ((v1, t1, u1), (v2, t2, u2)):
            target[...] = source[...].T
            swapped[0:EDGES] = -target[EDGES : 2 * EDGES]
            swapped[EDGES : 2 * EDGES] = target[0:EDGES]

    def far_frame(at):
        if at == 1:
            for copy in arrivals[1]:
                copy.wait_recv()
        expand(far_wigner.at[at], far_blocks)
        hot = far_hot[at]

        def far_gather(i):
            rows_p[wide(i)] = contract(far_grad[at, :, wide(i)], hot, 0, 0).astype(BF16)

        for i in range(7):
            far_gather(i)
        frame = (rows_p, p0.at[at], p1.at[at], p2.at[at])
        steps(8, lambda i: rotate_into(i, (frame,), far_blocks))
        swap(p1.at[at], q1.at[at])
        swap(p2.at[at], q2.at[at])

    arrivals = {0: grad_copies[0:3], 2: grad_copies[3:6], 1: []}

    def relay_targets():
        for copy in grad_copies:
            copy.wait_recv()
        for ref, rows in ((far_grad, ATOMS // 2), (far_wigner, WIG_READ // 2), (far_hot, ATOMS // 2)):
            for at, first in ((0, 0), (2, rows)):
                source, target = (ref.at[i, pl.ds(first, rows)] for i in (at, 1))
                arrivals[1].append(send(source, target, along_y[at]))

    forward_raw(1)
    partials(1)
    relay_targets()
    far_frame(0)
    forward_raw(2)
    partials(2)
    finish_mix(0)
    far_frame(2)
    forward_raw(3)
    partials(3)
    finish_mix(1)
    spread_far(0)
    relay_mix(0, True)
    forward_raw(4)
    partials(4)
    finish_mix(2)
    spread_far(1)
    relay_mix(0, False)
    relay_mix(1, True)
    forward_raw(5)
    partials(5)
    finish_mix(3)
    spread_far(2)
    relay_mix(1, False)
    relay_mix(2, True)
    turn_frames()
    far_frame(1)
    finish_mix(4)
    spread_far(3)
    relay_mix(2, False)
    relay_mix(3, True)
    for copy in v_copies:
        copy.wait_recv()
    weight_grads(0)
    finish_mix(5)
    spread_far(4)
    relay_mix(3, False)
    relay_mix(4, True)
    weight_grads(1)
    spread_far(5)
    relay_mix(4, False)
    relay_mix(5, True)
    weight_grads(2)
    relay_mix(5, False)

    def convolve(k):
        for i, piece in enumerate(PIECES):
            if piece[0] == k:
                for copy in b_relay[i, True] + b_relay[i, False]:
                    copy.wait_recv()
        width = COLS[k]
        if k == 0:
            weight = mix0[...].reshape(width, width)
            v0[...] = jnp.dot(t0[...], weight, preferred_element_type=F32).T.astype(BF16)
            d0[...] = jnp.dot(weight, d0[...], preferred_element_type=F32).astype(BF16)
            return
        t, u, v, d, s = ((t1, u1, v1, d1, s1), (t2, u2, v2, d2, s2))[k - 1]
        real = mix[k][0].reshape(width, width)
        imag = mix[k][1].reshape(width, width)
        result = jnp.dot(t[...], real, preferred_element_type=F32)
        result = result + jnp.dot(u[...], imag, preferred_element_type=F32)
        v[...] = result.T.astype(BF16)
        result = jnp.dot(real, d[...], preferred_element_type=F32)
        d[...] = (result + jnp.dot(imag, s[...], preferred_element_type=F32)).astype(BF16)

    for copy in v_copies:
        copy.wait_send()
    convolve(0)
    convolve(1)
    convolve(2)

    def rotate_back(target, f0, f1, f2):
        def body(i):
            for degree in range(LMAX + 1):
                extent, kept = 2 * degree + 1, min(degree, MMAX)
                rows = []
                for order in range(-kept, kept + 1):
                    source = (f0, f1, f2)[abs(order)]
                    rs = pl.ds(pl.multiple_of((degree - abs(order)) * 128 + i * 16, 16), 16)
                    lanes = slice(EDGES, 2 * EDGES) if order < 0 else slice(0, EDGES)
                    rows.append(source[rs, lanes].astype(F32).reshape(2, 8, EDGES))
                for n in range(extent):
                    total = None
                    for j, row in enumerate(rows):
                        term = blocks[degree][j, n][None] * row
                        total = term if total is None else total + term
                    first = (degree * degree + n) * 128
                    target[pl.ds(pl.multiple_of(first + i * 16, 16), 16)] = total.reshape(
                        16, EDGES
                    ).astype(BF16)

        steps(8, body)

    rotate_back(rows_b, d0, d1, d2)

    def scatter_back(i):
        total = contract(hot_source, rows_b[wide(i)], 1, 1)
        table_own[:, wide(i)] = total[0:ATOMS]
        table_ghost[:, wide(i)] = total[ATOMS : ATOMS + 2 * GHOSTS]

    for i in range(7):
        scatter_back(i)
    for side in range(2):
        mine = table_ghost[side * GHOSTS : (side + 1) * GHOSTS]
        back_send[side] = jnp.concatenate([mine[:, :PACK], mine[:, WIDTH - PACK :]], 0).astype(BF16)
    back_copies = [
        send(back_send.at[0], back_recv.at[0], to_prev),
        send(back_send.at[1], back_recv.at[1], to_next),
    ]

    rotate_back(rows_f, v0, v1, v2)

    def scatter(i):
        total = contract(hot_target, rows_f[wide(i)], 1, 1)
        updated[:, wide(i)] = (
            features[:, wide(i)].astype(F32) + MESSAGE_SCALE * total
        ).astype(BF16)

    for i in range(7):
        scatter(i)

    for k in range(3):
        finish_grads(k)

    for copy in back_copies:
        copy.wait_recv()
    came = [back_recv[side].astype(F32) for side in range(2)]
    for low, high, first, cut in ((0, PACK, 0, 0), (PACK, WIDTH, GHOSTS, 2 * PACK - WIDTH)):
        both = [a[first : first + GHOSTS, cut : cut + high - low] for a in came]
        both = jnp.concatenate(both, 0).astype(BF16)
        total = grad_out[:, low:high].astype(F32) + table_own[:, low:high]
        total = total + jnp.dot(spots, both, preferred_element_type=F32)
        grad_features[:, low:high] = total.astype(BF16)

    for copy in copies:
        if not any(copy is other for other in v_copies):
            copy.wait_send()


def copy_out(*refs):
    copies = [pltpu.make_async_copy(refs[i], refs[5 + i], refs[10].at[i]) for i in range(5)]
    for copy in copies:
        copy.start()
    for copy in copies:
        copy.wait()


def on_device(
    features, grad_out, wigner, sources, targets, ghost_index, edge_count, mixture,
    w_zero, w_one, w_two,
):
    def buffers(*lead, kind=BF16):
        shapes = []
        for k in range(3):
            mats = () if k == 0 else (2,)
            shapes.append(pltpu.VMEM(mats + lead + (ROWS[k], COLS[k]), kind))
        return shapes

    raw = [
        pltpu.VMEM((3, 2) + (() if k == 0 else (2,)) + (ROWS[k], COLS[k]), BF16) for k in range(3)
    ]
    frame = [
        pltpu.VMEM((896, EDGES), BF16),
        pltpu.VMEM((768, 2 * EDGES), BF16),
        pltpu.VMEM((640, 2 * EDGES), BF16),
    ]
    far_frames = [
        pltpu.VMEM((3, 896, EDGES), BF16),
        pltpu.VMEM((3, 768, 2 * EDGES), BF16),
        pltpu.VMEM((3, 640, 2 * EDGES), BF16),
    ]
    turned = [
        pltpu.VMEM((EDGES, 896), BF16),
        pltpu.VMEM((2 * EDGES, 768), BF16),
        pltpu.VMEM((2 * EDGES, 640), BF16),
    ]
    exchange = [pltpu.VMEM((2, 2 * GHOSTS, PACK), BF16)] * 4
    scratch = (
        raw
        + buffers(4)
        + buffers(3)
        + buffers(2, 4)
        + buffers(2, kind=F32)
        + buffers() * 2
        + [
            pltpu.VMEM((3, ATOMS, WIDTH), BF16),
            pltpu.VMEM((3, WIG_READ, EDGES), BF16),
            pltpu.VMEM((ATOMS, EDGES), BF16),
            pltpu.VMEM((3, ATOMS, EDGES), BF16),
            pltpu.VMEM((3, 2, 112, EDGES), BF16),
            pltpu.VMEM((3, 2, 96, 2 * EDGES), BF16),
            pltpu.VMEM((3, 2, 80, 2 * EDGES), BF16),
        ]
        + exchange
        + [pltpu.VMEM((WIG_READ, EDGES), F32)]
        + [
            pltpu.VMEM((2 * min(degree, MMAX) + 1, 2 * degree + 1, 8, EDGES), F32)
            for degree in range(LMAX + 1)
        ]
        * 2
        + [pltpu.VMEM((ATOMS + 2 * GHOSTS, WIDTH), BF16)]
        + [pltpu.VMEM((WIDTH, EDGES), BF16)] * 3
        + frame * 2
        + far_frames
        + frame[1:]
        + far_frames[1:]
        + turned
        + turned[1:]
        + [pltpu.VMEM((ATOMS, WIDTH), F32), pltpu.VMEM((2 * GHOSTS, WIDTH), F32)]
        + [pltpu.SemaphoreType.DMA((COPIES,))] * 2
    )
    vmem = pl.BlockSpec(memory_space=pltpu.VMEM)
    smem = pl.BlockSpec(memory_space=pltpu.SMEM)
    results = pl.pallas_call(
        kernel,
        out_shape=(
            jax.ShapeDtypeStruct((ATOMS, WIDTH), BF16),
            jax.ShapeDtypeStruct((ATOMS, WIDTH), BF16),
            jax.ShapeDtypeStruct((1, 112, 896), BF16),
            jax.ShapeDtypeStruct((1, 2, 96, 768), BF16),
            jax.ShapeDtypeStruct((1, 2, 80, 640), BF16),
        ),
        in_specs=[smem, smem] + [vmem] * 9,
        out_specs=(vmem,) * 5,
        scratch_shapes=scratch,
        compiler_params=pltpu.CompilerParams(
            collective_id=0, has_side_effects=True, vmem_limit_bytes=58 * 1024 * 1024
        ),
        name="message_layer",
    )(
        mixture,
        edge_count,
        features,
        grad_out,
        wigner,
        sources.reshape(1, -1),
        targets.reshape(1, -1),
        ghost_index,
        w_zero,
        w_one,
        w_two,
    )
    anywhere = pl.BlockSpec(memory_space=pl.ANY)
    return pl.pallas_call(
        copy_out,
        out_shape=tuple(jax.ShapeDtypeStruct(a.shape, a.dtype) for a in results),
        in_specs=[vmem] * 5,
        out_specs=(anywhere,) * 5,
        scratch_shapes=[pltpu.SemaphoreType.DMA((5,))],
        name="copy_out",
    )(*results)


def solution(mesh):
    both = ("dp", "space")
    return jax.shard_map(
        on_device,
        mesh=mesh,
        in_specs=(
            P(both, None),
            P(both, None),
            P(None, both),
            P(both),
            P(both),
            P(both, None, None),
            P("dp", "space"),
            P(),
            P("dp", "space", None),
            P("dp", None, "space", None),
            P("dp", None, "space", None),
        ),
        out_specs=(
            P(both, None),
            P(both, None),
            P("dp", "space", None),
            P("dp", None, "space", None),
            P("dp", None, "space", None),
        ),
        check_vma=False,
    )
```

```python
import functools

import jax
import jax.numpy as jnp
from jax import lax
from jax.experimental import pallas as pl
from jax.experimental.pallas import tpu as pltpu
from jax.sharding import PartitionSpec as P

BF16 = jnp.bfloat16
F32 = jnp.float32
MESH = pl.DeviceIdType.MESH

LMAX = 6
MMAX = 2
EDGES = 128
ATOMS = 32
GHOSTS = 8
WIDTH = 6272
PACK = 3200
WIG_READ = 416
MESSAGE_SCALE = 0.25
WEIGHT_SCALE = 1024.0 ** -0.5

ROWS = (112, 96, 80)
COLS = (896, 768, 640)
MATS = (1, 2, 2)
PIECES = (
    (0, 0, 0, 48, 32),
    (0, 0, 48, 64, 32),
    (1, 0, 0, 96, 48),
    (1, 1, 0, 96, 48),
    (2, 0, 0, 80, 32),
    (2, 1, 0, 80, 48),
)
COPIES = 192


def contract(left, right, left_dim, right_dim):
    return lax.dot_general(
        left, right, (((left_dim,), (right_dim,)), ((), ())), preferred_element_type=F32
    )


def view(ref, piece, lead, first=0, rows=None):
    k, mat, start, length, _ = piece
    rs = pl.ds(start + first, length if rows is None else rows)
    return ref.at[lead + (rs,)] if k == 0 else ref.at[(mat,) + lead + (rs,)]


def experts(ref, piece, lead=()):
    k, mat, start, length, _ = piece
    lead = lead + (slice(None),)
    return ref.at[lead + (pl.ds(start, length),)] if k == 0 else ref.at[lead + (mat,)]


def steps(count, body):
    def step(i, carry):
        body(i)
        return carry

    lax.fori_loop(0, count, step, 0)


def tiles16(i):
    return pl.ds(pl.multiple_of(i * 16, 16), 16)


def kernel(
    mixture, count, features, grad_out, wigner, sources, targets, ghost_index, w0, w1, w2,
    updated, grad_features, out0, out1, out2,
    raw0, raw1, raw2, par0, par1, par2, za0, za1, za2, mix0, mix1, mix2,
    keep0, keep1, keep2, cs0, cs1, cs2, cx0, cx1, cx2,
    far_grad, far_wigner, hot_send, far_hot, far_v0, far_v1, far_v2,
    ghost_send, ghost_recv, back_send, back_recv,
    wig32, blk0, blk1, blk2, blk3, blk4, blk5, blk6, fbk0, fbk1, fbk2, fbk3, fbk4, fbk5, fbk6,
    table, rows_f, rows_b, rows_p, v0, v1, v2, d0, d1, d2, p0, p1, p2, s1, s2, q1, q2, t0, t1, t2, u1, u2,
    table_own, table_ghost, send_sem, recv_sem,
):
    w = (w0, w1, w2)
    raw = (raw0, raw1, raw2)
    par = (par0, par1, par2)
    za = (za0, za1, za2)
    mix = (mix0, mix1, mix2)
    keep, cs, cx = (keep0, keep1, keep2), (cs0, cs1, cs2), (cx0, cx1, cx2)
    far_v = (far_v0, far_v1, far_v2)
    out = (out0, out1, out2)
    blocks = (blk0, blk1, blk2, blk3, blk4, blk5, blk6)
    far_blocks = (fbk0, fbk1, fbk2, fbk3, fbk4, fbk5, fbk6)

    dp, sp = lax.axis_index("dp"), lax.axis_index("space")
    core, z, xl = dp % 2, (dp // 2) % 4, dp // 8
    y, xh = sp % 4, sp // 4
    dp_core = dp + 1 - 2 * core
    dp_x = (1 - xl) * 8 + z * 2 + core
    dp_xc = (1 - xl) * 8 + z * 2 + 1 - core
    sp_x = (1 - xh) * 4 + y

    def at_z(step):
        return xl * 8 + ((z + step) % 4) * 2 + core

    def at_y(step):
        return xh * 4 + (y + step) % 4

    to_core, to_x = (dp_core, sp), (dp_x, sp)
    along_z = tuple((at_z(step), sp) for step in (1, 2, 3))
    along_y = tuple((dp, at_y(step)) for step in (1, 2, 3))
    to_far = (dp, sp_x)
    to_next, to_prev = (dp, (sp + 1) % 8), (dp, (sp + 7) % 8)
    partners = (to_core, to_x, to_far, to_next, to_prev) + along_z + along_y

    barrier = pltpu.get_barrier_semaphore()
    for partner in partners:
        pl.semaphore_signal(barrier, inc=1, device_id=partner, device_id_type=MESH)

    copies = []

    def send(source, target, device):
        index = len(copies)
        copy = pltpu.make_async_remote_copy(
            src_ref=source,
            dst_ref=target,
            send_sem=send_sem.at[index],
            recv_sem=recv_sem.at[index],
            device_id=device,
            device_id_type=MESH,
        )
        copy.start()
        copies.append(copy)
        return copy

    atom = lax.broadcasted_iota(jnp.int32, (ATOMS, GHOSTS), 0)
    spots = jnp.concatenate(
        [(atom == ghost_index[0, side : side + 1]).astype(F32) for side in range(2)], 1
    )
    ghosts = jnp.dot(spots.T.astype(BF16), features[...], preferred_element_type=F32)
    spots = spots.astype(BF16)
    for side in range(2):
        mine = ghosts[side * GHOSTS : (side + 1) * GHOSTS]
        ghost_send[side] = jnp.concatenate([mine[:, :PACK], mine[:, WIDTH - PACK :]], 0).astype(BF16)

    live = lax.broadcasted_iota(jnp.int32, (ATOMS, EDGES), 1) < count[0, 0]
    hot_target = (
        (lax.broadcasted_iota(jnp.int32, (ATOMS, EDGES), 0) == targets[...]) & live
    ).astype(F32)
    hot_quarter = (MESSAGE_SCALE * hot_target).astype(BF16)
    hot_target = hot_target.astype(BF16)
    hot_source = (
        lax.broadcasted_iota(jnp.int32, (ATOMS + 2 * GHOSTS, EDGES), 0) == sources[...]
    ).astype(BF16)

    hot_send[...] = hot_quarter

    pl.semaphore_wait(barrier, len(partners))

    ghost_copies = [
        send(ghost_send.at[0], ghost_recv.at[0], to_next),
        send(ghost_send.at[1], ghost_recv.at[1], to_prev),
    ]
    raw_x, raw_core, raw_xc = {}, {}, {}
    grad_copies = []
    for i, piece in enumerate(PIECES):
        k = piece[0]
        raw_x[i] = send(experts(w[k], piece), experts(raw[k], piece, (1,)), to_x)
        raw_core[i] = send(experts(w[k], piece), experts(raw[k], piece, (0,)), to_core)
        if i == 0:
            for at in (0, 2):
                grad_copies += [
                    send(grad_out, far_grad.at[at], along_y[at]),
                    send(wigner.at[0:WIG_READ], far_wigner.at[at], along_y[at]),
                    send(hot_send, far_hot.at[at], along_y[at]),
                ]

    def forward_raw(i):
        piece = PIECES[i]
        raw_x[i].wait_recv()
        here = raw[piece[0]]
        raw_xc[i] = send(experts(here, piece, (1,)), experts(here, piece, (2,)), to_core)

    z_sums = {}

    def partials(i):
        piece = PIECES[i]
        k, mat, start, length, _ = piece
        raw_core[i].wait_recv()
        raw_xc[i].wait_recv()
        across = COLS[k] // 128
        scale = [
            [
                mixture[(xl * 4 + (z + step) % 4) * 2 + core, 2 * owner + i]
                for owner in (dp, dp_core, dp_x, dp_xc)
                for i in range(2)
            ]
            for step in range(4)
        ]
        lead = () if k == 0 else (mat,)

        def body(t):
            rs = pl.ds(pl.multiple_of(start + t * 16, 16), 16)
            for block in range(across):
                c = slice(block * 128, (block + 1) * 128)
                terms = [w[k][(i,) + lead + (rs, c)].astype(F32) for i in range(2)]
                for slot in range(3):
                    terms += [raw[k][(slot, i) + lead + (rs, c)].astype(F32) for i in range(2)]
                for step in range(4):
                    total = scale[step][0] * terms[0]
                    for factor, term in zip(scale[step][1:], terms[1:]):
                        total = total + factor * term
                    par[k][lead + (step, rs, c)] = total.astype(BF16)

        steps(length // 16, body)
        z_sums[i] = [
            send(view(par[k], piece, (at + 1,)), view(za[k], piece, (at,)), along_z[at])
            for at in (1, 0, 2)
        ]

    def add_up(target, terms, rows, kind=BF16):
        def body(i):
            rs = tiles16(i)
            total = terms[0][rs].astype(F32)
            for term in terms[1:]:
                total = total + term[rs].astype(F32)
            target[rs] = total.astype(kind)

        steps(rows // 16, body)

    def matrix(ref, k, mat, lead):
        return ref.at[lead] if k == 0 else ref.at[(mat,) + lead]

    b_far, b_along = {}, {}

    def spread(i, own):
        piece = PIECES[i]
        here = view(mix[piece[0]], piece, (xh if own else 1 - xh, y))
        b_along[i, own] = [send(here, here, along_y[at]) for at in (0, 2)]

    def finish_mix(i):
        piece = PIECES[i]
        k = piece[0]
        for copy in z_sums[i]:
            copy.wait_recv()
        here = view(mix[k], piece, (xh, y))
        terms = [view(par[k], piece, (0,))] + [view(za[k], piece, (at,)) for at in range(3)]
        add_up(here, terms, piece[3])
        b_far[i] = send(here, here, to_far)
        spread(i, True)

    def spread_far(i):
        b_far[i].wait_recv()
        spread(i, False)

    b_relay = {}

    def relay_mix(i, own):
        piece = PIECES[i]
        k, _, _, length, upward = piece
        place = xh if own else 1 - xh
        b_relay[i, own] = []
        for copy in b_along[i, own]:
            copy.wait_recv()
        for at, step, first, rows in ((0, 3, 0, upward), (2, 1, upward, length - upward)):
            here = view(mix[k], piece, (place, (y + step) % 4), first, rows)
            b_relay[i, own].append(send(here, here, along_y[at]))

    v_copies = []
    c_far = {}

    def send_rows():
        for k, source in enumerate((v0, v1, v2)):
            rows = ROWS[k]
            for at in (0, 2, 1):
                for side in range(2):
                    first = (side * 4 + (y + at + 1) % 4) * rows
                    part = source.at[pl.ds(pl.multiple_of(first, 16), rows)]
                    v_copies.append(send(part, far_v[k].at[at, side], along_y[at]))

    def weight_grads(k):
        rows = ROWS[k]
        v, d, p = ((v0, d0, p0), (v1, d1, p1), (v2, d2, p2))[k]
        swapped = (None, (s1, q1), (s2, q2))[k]
        own = [v[pl.ds(pl.multiple_of((side * 4 + y) * rows, 16), rows)] for side in range(2)]
        own = jnp.concatenate(own, 0)
        others = [far_v[k][at].reshape(2 * rows, own.shape[1]) for at in range(3)]
        for mat in range(MATS[k]):
            near, far = (d, p) if mat == 0 else swapped
            total = contract(own, near[...], 1, 1)
            for at in range(3):
                total = total + contract(others[at], far[at], 1, 1)
            total = (WEIGHT_SCALE * total).reshape(2, rows, COLS[k])
            for side in range(2):
                matrix(keep[k], k, mat, (side,))[...] = total[side]
            matrix(cs[k], k, mat, ())[...] = matrix(keep[k], k, mat, (1 - xh,))[...].astype(BF16)
        c_far[k] = send(cs[k], cx[k], to_far)

    def finish_grads(k):
        c_far[k].wait_recv()
        for mat in range(MATS[k]):
            target = out[k].at[(0,) if k == 0 else (0, mat)]
            add_up(target, [matrix(keep[k], k, mat, (xh,)), matrix(cx[k], k, mat, ())], ROWS[k])

    def expand(matrix, target):
        wig32[...] = matrix[0:WIG_READ].astype(F32)
        for degree in range(LMAX + 1):
            extent, kept = 2 * degree + 1, min(degree, MMAX)
            start = degree * (2 * degree - 1) * (2 * degree + 1) // 3 + (degree - kept) * extent
            for j in range(2 * kept + 1):
                rows = wig32[start + j * extent : start + (j + 1) * extent]
                target[degree][j] = jnp.broadcast_to(rows[:, None, :], (extent, 8, EDGES))

    expand(wigner, blocks)

    def wide(i):
        return slice(i * 896, (i + 1) * 896)

    def back_gather(i):
        rows_b[wide(i)] = contract(grad_out[:, wide(i)], hot_quarter, 0, 0).astype(BF16)

    for i in range(7):
        back_gather(i)

    for copy in ghost_copies:
        copy.wait_recv()
    table[0:ATOMS] = features[...]
    came = [ghost_recv[side].astype(F32) for side in range(2)]
    for low, high, first, cut in ((0, PACK, 0, 0), (PACK, WIDTH, GHOSTS, 2 * PACK - WIDTH)):
        both = [a[first : first + GHOSTS, cut : cut + high - low] for a in came]
        table[ATOMS : ATOMS + 2 * GHOSTS, low:high] = jnp.concatenate(both, 0).astype(BF16)

    def gather(i):
        rows_f[wide(i)] = contract(table[:, wide(i)], hot_source, 0, 0).astype(BF16)

    for i in range(7):
        gather(i)

    def rotate_into(i, frames, matrices):
        for source, f0, f1, f2 in frames:
            for degree in range(LMAX + 1):
                kept = min(degree, MMAX)
                total = None
                for n in range(2 * degree + 1):
                    first = (degree * degree + n) * 128
                    row = source[pl.ds(pl.multiple_of(first + i * 16, 16), 16)].astype(F32)
                    factor = matrices[degree][:, n]
                    term = factor[:, None] * row.reshape(1, 2, 8, EDGES)
                    total = term if total is None else total + term
                result = total.reshape(2 * kept + 1, 16, EDGES).astype(BF16)
                f0[pl.ds(pl.multiple_of(degree * 128 + i * 16, 16), 16)] = result[kept]
                for order, target in ((1, f1), (2, f2)):
                    if kept >= order:
                        rs = pl.ds(pl.multiple_of((degree - order) * 128 + i * 16, 16), 16)
                        target[rs, 0:EDGES] = result[kept + order]
                        target[rs, EDGES : 2 * EDGES] = result[kept - order]

    forward_raw(0)
    partials(0)
    steps(8, lambda i: rotate_into(i, ((rows_f, v0, v1, v2), (rows_b, d0, d1, d2)), blocks))
    send_rows()
    def swap(source, target):
        target[:, 0:EDGES] = source[:, EDGES : 2 * EDGES]
        target[:, EDGES : 2 * EDGES] = -source[:, 0:EDGES]

    def turn_frames():
        swap(d1, s1)
        swap(d2, s2)
        t0[...] = v0[...].T
        for source, target, swapped in ((v1, t1, u1), (v2, t2, u2)):
            target[...] = source[...].T
            swapped[0:EDGES] = -target[EDGES : 2 * EDGES]
            swapped[EDGES : 2 * EDGES] = target[0:EDGES]

    def far_frame(at):
        if at == 1:
            for copy in arrivals[1]:
                copy.wait_recv()
        expand(far_wigner.at[at], far_blocks)
        hot = far_hot[at]

        def far_gather(i):
            rows_p[wide(i)] = contract(far_grad[at, :, wide(i)], hot, 0, 0).astype(BF16)

        for i in range(7):
            far_gather(i)
        frame = (rows_p, p0.at[at], p1.at[at], p2.at[at])
        steps(8, lambda i: rotate_into(i, (frame,), far_blocks))
        swap(p1.at[at], q1.at[at])
        swap(p2.at[at], q2.at[at])

    arrivals = {0: grad_copies[0:3], 2: grad_copies[3:6], 1: []}

    def relay_targets():
        for copy in grad_copies:
            copy.wait_recv()
        for ref, rows in ((far_grad, ATOMS // 2), (far_wigner, WIG_READ // 2), (far_hot, ATOMS // 2)):
            for at, first in ((0, 0), (2, rows)):
                source, target = (ref.at[i, pl.ds(first, rows)] for i in (at, 1))
                arrivals[1].append(send(source, target, along_y[at]))

    forward_raw(1)
    partials(1)
    relay_targets()
    far_frame(0)
    forward_raw(2)
    partials(2)
    finish_mix(0)
    far_frame(2)
    forward_raw(3)
    partials(3)
    finish_mix(1)
    spread_far(0)
    relay_mix(0, True)
    forward_raw(4)
    partials(4)
    finish_mix(2)
    spread_far(1)
    relay_mix(0, False)
    relay_mix(1, True)
    forward_raw(5)
    partials(5)
    finish_mix(3)
    spread_far(2)
    relay_mix(1, False)
    relay_mix(2, True)
    turn_frames()
    far_frame(1)
    finish_mix(4)
    spread_far(3)
    relay_mix(2, False)
    relay_mix(3, True)
    for copy in v_copies:
        copy.wait_recv()
    weight_grads(0)
    finish_mix(5)
    spread_far(4)
    relay_mix(3, False)
    relay_mix(4, True)
    weight_grads(1)
    spread_far(5)
    relay_mix(4, False)
    relay_mix(5, True)
    weight_grads(2)
    relay_mix(5, False)

    def convolve(k):
        for i, piece in enumerate(PIECES):
            if piece[0] == k:
                for copy in b_relay[i, True] + b_relay[i, False]:
                    copy.wait_recv()
        width = COLS[k]
        if k == 0:
            weight = mix0[...].reshape(width, width)
            v0[...] = jnp.dot(t0[...], weight, preferred_element_type=F32).T.astype(BF16)
            d0[...] = jnp.dot(weight, d0[...], preferred_element_type=F32).astype(BF16)
            return
        t, u, v, d, s = ((t1, u1, v1, d1, s1), (t2, u2, v2, d2, s2))[k - 1]
        real = mix[k][0].reshape(width, width)
        imag = mix[k][1].reshape(width, width)
        result = jnp.dot(t[...], real, preferred_element_type=F32)
        result = result + jnp.dot(u[...], imag, preferred_element_type=F32)
        v[...] = result.T.astype(BF16)
        result = jnp.dot(real, d[...], preferred_element_type=F32)
        d[...] = (result + jnp.dot(imag, s[...], preferred_element_type=F32)).astype(BF16)

    for copy in v_copies:
        copy.wait_send()
    convolve(0)
    convolve(1)
    convolve(2)

    def rotate_back(target, f0, f1, f2):
        def body(i):
            for degree in range(LMAX + 1):
                extent, kept = 2 * degree + 1, min(degree, MMAX)
                rows = []
                for order in range(-kept, kept + 1):
                    source = (f0, f1, f2)[abs(order)]
                    rs = pl.ds(pl.multiple_of((degree - abs(order)) * 128 + i * 16, 16), 16)
                    lanes = slice(EDGES, 2 * EDGES) if order < 0 else slice(0, EDGES)
                    rows.append(source[rs, lanes].astype(F32).reshape(2, 8, EDGES))
                for n in range(extent):
                    total = None
                    for j, row in enumerate(rows):
                        term = blocks[degree][j, n][None] * row
                        total = term if total is None else total + term
                    first = (degree * degree + n) * 128
                    target[pl.ds(pl.multiple_of(first + i * 16, 16), 16)] = total.reshape(
                        16, EDGES
                    ).astype(BF16)

        steps(8, body)

    rotate_back(rows_b, d0, d1, d2)

    def scatter_back(i):
        total = contract(hot_source, rows_b[wide(i)], 1, 1)
        table_own[:, wide(i)] = total[0:ATOMS]
        table_ghost[:, wide(i)] = total[ATOMS : ATOMS + 2 * GHOSTS]

    for i in range(7):
        scatter_back(i)
    for side in range(2):
        mine = table_ghost[side * GHOSTS : (side + 1) * GHOSTS]
        back_send[side] = jnp.concatenate([mine[:, :PACK], mine[:, WIDTH - PACK :]], 0).astype(BF16)
    back_copies = [
        send(back_send.at[0], back_recv.at[0], to_prev),
        send(back_send.at[1], back_recv.at[1], to_next),
    ]

    rotate_back(rows_f, v0, v1, v2)

    def scatter(i):
        total = contract(hot_target, rows_f[wide(i)], 1, 1)
        updated[:, wide(i)] = (
            features[:, wide(i)].astype(F32) + MESSAGE_SCALE * total
        ).astype(BF16)

    for i in range(7):
        scatter(i)

    for k in range(3):
        finish_grads(k)

    for copy in back_copies:
        copy.wait_recv()
    came = [back_recv[side].astype(F32) for side in range(2)]
    for low, high, first, cut in ((0, PACK, 0, 0), (PACK, WIDTH, GHOSTS, 2 * PACK - WIDTH)):
        both = [a[first : first + GHOSTS, cut : cut + high - low] for a in came]
        both = jnp.concatenate(both, 0).astype(BF16)
        total = grad_out[:, low:high].astype(F32) + table_own[:, low:high]
        total = total + jnp.dot(spots, both, preferred_element_type=F32)
        grad_features[:, low:high] = total.astype(BF16)

    for copy in copies:
        if not any(copy is other for other in v_copies):
            copy.wait_send()


def copy_out(*refs):
    copies = [pltpu.make_async_copy(refs[i], refs[5 + i], refs[10].at[i]) for i in range(5)]
    for copy in copies:
        copy.start()
    for copy in copies:
        copy.wait()


def on_device(
    features, grad_out, wigner, sources, targets, ghost_index, edge_count, mixture,
    w_zero, w_one, w_two,
):
    def buffers(*lead, kind=BF16):
        shapes = []
        for k in range(3):
            mats = () if k == 0 else (2,)
            shapes.append(pltpu.VMEM(mats + lead + (ROWS[k], COLS[k]), kind))
        return shapes

    raw = [
        pltpu.VMEM((3, 2) + (() if k == 0 else (2,)) + (ROWS[k], COLS[k]), BF16) for k in range(3)
    ]
    frame = [
        pltpu.VMEM((896, EDGES), BF16),
        pltpu.VMEM((768, 2 * EDGES), BF16),
        pltpu.VMEM((640, 2 * EDGES), BF16),
    ]
    far_frames = [
        pltpu.VMEM((3, 896, EDGES), BF16),
        pltpu.VMEM((3, 768, 2 * EDGES), BF16),
        pltpu.VMEM((3, 640, 2 * EDGES), BF16),
    ]
    turned = [
        pltpu.VMEM((EDGES, 896), BF16),
        pltpu.VMEM((2 * EDGES, 768), BF16),
        pltpu.VMEM((2 * EDGES, 640), BF16),
    ]
    exchange = [pltpu.VMEM((2, 2 * GHOSTS, PACK), BF16)] * 4
    scratch = (
        raw
        + buffers(4)
        + buffers(3)
        + buffers(2, 4)
        + buffers(2, kind=F32)
        + buffers() * 2
        + [
            pltpu.VMEM((3, ATOMS, WIDTH), BF16),
            pltpu.VMEM((3, WIG_READ, EDGES), BF16),
            pltpu.VMEM((ATOMS, EDGES), BF16),
            pltpu.VMEM((3, ATOMS, EDGES), BF16),
            pltpu.VMEM((3, 2, 112, EDGES), BF16),
            pltpu.VMEM((3, 2, 96, 2 * EDGES), BF16),
            pltpu.VMEM((3, 2, 80, 2 * EDGES), BF16),
        ]
        + exchange
        + [pltpu.VMEM((WIG_READ, EDGES), F32)]
        + [
            pltpu.VMEM((2 * min(degree, MMAX) + 1, 2 * degree + 1, 8, EDGES), F32)
            for degree in range(LMAX + 1)
        ]
        * 2
        + [pltpu.VMEM((ATOMS + 2 * GHOSTS, WIDTH), BF16)]
        + [pltpu.VMEM((WIDTH, EDGES), BF16)] * 3
        + frame * 2
        + far_frames
        + frame[1:]
        + far_frames[1:]
        + turned
        + turned[1:]
        + [pltpu.VMEM((ATOMS, WIDTH), F32), pltpu.VMEM((2 * GHOSTS, WIDTH), F32)]
        + [pltpu.SemaphoreType.DMA((COPIES,))] * 2
    )
    vmem = pl.BlockSpec(memory_space=pltpu.VMEM)
    smem = pl.BlockSpec(memory_space=pltpu.SMEM)
    results = pl.pallas_call(
        kernel,
        out_shape=(
            jax.ShapeDtypeStruct((ATOMS, WIDTH), BF16),
            jax.ShapeDtypeStruct((ATOMS, WIDTH), BF16),
            jax.ShapeDtypeStruct((1, 112, 896), BF16),
            jax.ShapeDtypeStruct((1, 2, 96, 768), BF16),
            jax.ShapeDtypeStruct((1, 2, 80, 640), BF16),
        ),
        in_specs=[smem, smem] + [vmem] * 9,
        out_specs=(vmem,) * 5,
        scratch_shapes=scratch,
        compiler_params=pltpu.CompilerParams(
            collective_id=0, has_side_effects=True, vmem_limit_bytes=58 * 1024 * 1024
        ),
        name="message_layer",
    )(
        mixture,
        edge_count,
        features,
        grad_out,
        wigner,
        sources.reshape(1, -1),
        targets.reshape(1, -1),
        ghost_index,
        w_zero,
        w_one,
        w_two,
    )
    anywhere = pl.BlockSpec(memory_space=pl.ANY)
    return pl.pallas_call(
        copy_out,
        out_shape=tuple(jax.ShapeDtypeStruct(a.shape, a.dtype) for a in results),
        in_specs=[vmem] * 5,
        out_specs=(anywhere,) * 5,
        scratch_shapes=[pltpu.SemaphoreType.DMA((5,))],
        name="copy_out",
    )(*results)


def solution(mesh):
    both = ("dp", "space")
    return jax.shard_map(
        on_device,
        mesh=mesh,
        in_specs=(
            P(both, None),
            P(both, None),
            P(None, both),
            P(both),
            P(both),
            P(both, None, None),
            P("dp", "space"),
            P(),
            P("dp", "space", None),
            P("dp", None, "space", None),
            P("dp", None, "space", None),
        ),
        out_specs=(
            P(both, None),
            P(both, None),
            P("dp", "space", None),
            P("dp", None, "space", None),
            P("dp", None, "space", None),
        ),
        check_vma=False,
    )
```
